768 devices in a mesh: dom: 12 (over z), work: 64 (over y, x, core).
Axes of the slice: x: 4, y: 8, z: 12, core: 2. Of those that a mesh axis runs over, the one named last changes fastest.
Arguments:
- embeddings: float32 [12288, 400], P(('dom', 'work'))
- adagrad: float32 [12288], P(('dom', 'work')), may hold values from 0.05 to 1
- plan: int32 [12], replicated, may hold values from 0 to 11, each once
- src_ids: int32 [12, 64, 512], P('dom', 'work'), may hold values from 0 to 1023
- dst_ids: int32 [12, 64, 512], P('dom', 'work'), may hold values from 0 to 1023
- neg_ids: int32 [12, 64, 512], P('dom', 'work'), may hold values from 0 to 511
- counts: int32 [12, 64], P('dom', 'work'), may hold values from 64 to 512, as said below
Outputs:
- new_embeddings: float32 [12288, 400], P(('dom', 'work'))
- new_adagrad: float32 [12288], P(('dom', 'work'))
The draws below stay inside these ranges and needn't reach their ends.
Inputs may be any that keep to these rules, and one draw needn't show every extreme that they name: plan is a permutation of the partitions. `counts`: some worker's block is full in every draw.
All inputs are finite; a program needn't handle non-finite values.
Results may differ from the reference program's by a relative error of at most 0.0003.
Values sent between devices are 32-bit elements; how exact they have to be, the bound alone decides.
No kernel may reach another device: no remote copies, remote signals or barrier semaphores. Data moves between devices by JAX's collectives and lax.ppermute only.
A program may use at most 32 MiB of HBM per device.

```python
import math
import jax
import jax.numpy as jnp
import numpy as np
from jax import lax

D = 400
BLOCK = 512
NEG = 512
PARTS_SIZE = 12
WORKERS = 64
PART_ROWS = 1024
ENTITIES = 12288


def draw_embeddings(key, part):
    key = jax.random.fold_in(key, 11)
    first = jax.random.fold_in(key, 0)
    values = 0.4 * jax.random.normal(first, (ENTITIES, D), jnp.float32)
    return values.astype(jnp.float32)


def draw_counts(key, part):
    key = jax.random.fold_in(key, 5)
    first, second = jax.random.split(key, 2)
    total = PARTS_SIZE * WORKERS
    values = jax.random.randint(first, (total,), BLOCK // 8, BLOCK + 1)
    spot = jax.random.randint(second, (), 0, total)
    values = jnp.where(jnp.arange(total, dtype=jnp.int32) == spot, BLOCK, values)
    return values.reshape(PARTS_SIZE, WORKERS).astype(jnp.int32)


def with_ends(array, own_key, low, high):
    longest = array.shape.index(max(array.shape))
    spots = []
    for shift in (0, 1):
        where = [jax.random.randint(jax.random.fold_in(own_key, axis), (), 0, length) for axis, length in enumerate(array.shape)]
        where[longest] = (where[longest] + shift) % array.shape[longest]
        spots.append(tuple(where))
    return array.at[spots[0]].set(low).at[spots[1]].set(high)


def level_of(own_key, extent, pieces, least, top_value):
    def one(axis_at, blocks):
        draws = jax.random.uniform(jax.random.fold_in(jax.random.fold_in(own_key, 6), axis_at), (blocks,), jnp.float32, least / len(pieces), top_value / len(pieces))
        return jnp.repeat(jnp.exp(draws), extent[axis_at] // blocks).reshape((-1,) + (1,) * (len(extent) - axis_at - 1))

    factor_of = one(*pieces[0])
    for cut in pieces[1:]:
        factor_of = factor_of * one(*cut)
    return factor_of


def rank_table(number_of, skew):
    loads = [(1 << 20) // math.isqrt(standing ** skew) + 1 for standing in range(1, number_of + 1)]
    width = 1 + sum(loads) // (1 << 30)
    return np.cumsum(np.array([max(1, weight // width) for weight in loads]))


def skewed_ids(rng, extent, amount, lean):
    table = rank_table(amount, lean)
    ticket = jax.random.randint(jax.random.fold_in(rng, 1), extent, 0, int(table[amount - 1]))
    rank = jnp.searchsorted(jnp.asarray(table, jnp.int32), ticket, side="right")
    return jax.random.permutation(jax.random.fold_in(rng, 2), amount)[rank].astype(jnp.int32)


def setup_inputs(seed: int = 0) -> dict:
    keys = jax.random.split(jax.random.key(seed), 8)
    return {
        "embeddings": draw_embeddings(jax.random.fold_in(keys[7], 71), 0),
        "adagrad": jnp.clip(jnp.exp(math.log(1.0) - 2.9957323 * jax.random.uniform(keys[1], (ENTITIES,), jnp.float32) ** level_of(keys[1], (ENTITIES,), ((0, 768),), -0.2, 0.2)), 0.05, 1.0),
        "plan": jax.random.permutation(keys[2], PARTS_SIZE).astype(jnp.int32),
        "src_ids": with_ends(jax.random.randint(keys[3], (PARTS_SIZE, WORKERS, BLOCK), 0, PART_ROWS), jax.random.fold_in(keys[3], 1), 0, PART_ROWS - 1).astype(jnp.int32),
        "dst_ids": with_ends(skewed_ids(keys[4], (PARTS_SIZE, WORKERS, BLOCK), PART_ROWS, 2), jax.random.fold_in(keys[4], 3), 0, PART_ROWS - 1).astype(jnp.int32),
        "neg_ids": with_ends(jax.random.randint(keys[5], (PARTS_SIZE, WORKERS, NEG), 0, BLOCK), jax.random.fold_in(keys[5], 1), 0, BLOCK - 1).astype(jnp.int32),
        "counts": draw_counts(jax.random.fold_in(keys[7], 71), 0),
    }


learn_rate = 0.1
epsilon = 1e-08

def block_grads(src_rows, dst_rows, neg_slots, live_count):
    slot_count = src_rows.shape[0]
    neg_rows = jnp.take(dst_rows, neg_slots, axis=0)
    positive = lax.optimization_barrier(jnp.sum(src_rows * dst_rows, axis=1))
    scores = jnp.dot(src_rows, neg_rows.T, precision=lax.Precision.HIGHEST, preferred_element_type=jnp.float32)
    logits = jnp.concatenate([positive[:, None], scores], axis=1)
    row_max = lax.optimization_barrier(jnp.max(logits, axis=1, keepdims=True))
    shifted = jnp.exp(logits - row_max)
    probabilities = shifted / lax.optimization_barrier(jnp.sum(shifted, axis=1, keepdims=True))
    live_mask = (jnp.arange(slot_count, dtype=jnp.int32) < live_count).astype(jnp.float32)
    pos_weight = (probabilities[:, 0] - 1.0) * live_mask
    neg_weight = probabilities[:, 1:] * live_mask[:, None]
    src_grad = pos_weight[:, None] * dst_rows + jnp.dot(neg_weight, neg_rows, precision=lax.Precision.HIGHEST, preferred_element_type=jnp.float32)
    neg_grad = jnp.dot(neg_weight.T, src_rows, precision=lax.Precision.HIGHEST, preferred_element_type=jnp.float32)
    dst_grad = pos_weight[:, None] * src_rows + jnp.zeros_like(dst_rows).at[neg_slots].add(neg_grad)
    return (src_grad, dst_grad)

def reference(embeddings, adagrad, plan, src_ids, dst_ids, neg_ids, counts):

    def accumulate(grads, flat_index):
        left_part = flat_index // WORKERS
        worker = flat_index % WORKERS
        right_part = plan[left_part]
        src_global = (left_part * PART_ROWS + src_ids[left_part, worker]).astype(jnp.int32)
        dst_global = (right_part * PART_ROWS + dst_ids[left_part, worker]).astype(jnp.int32)
        src_rows = jnp.take(embeddings, src_global, axis=0)
        dst_rows = jnp.take(embeddings, dst_global, axis=0)
        src_grad, dst_grad = block_grads(src_rows, dst_rows, neg_ids[left_part, worker], counts[left_part, worker])
        grads = grads.at[src_global].add(src_grad).at[dst_global].add(dst_grad)
        return (grads, None)
    start_grads = jnp.zeros((ENTITIES, D), jnp.float32)
    grads, unused = lax.scan(accumulate, start_grads, jnp.arange(PARTS_SIZE * WORKERS, dtype=jnp.int32))
    new_adagrad = adagrad + lax.optimization_barrier(jnp.mean(grads * grads, axis=1))
    new_embeddings = embeddings - learn_rate * grads / (jnp.sqrt(new_adagrad)[:, None] + epsilon)
    return (new_embeddings, new_adagrad)
```

```python
import jax
import jax.numpy as jnp
from jax import lax
from jax.experimental import pallas as pl
from jax.experimental.pallas import tpu as pltpu
from jax.sharding import Mesh, PartitionSpec as P

learn_rate = 0.1
epsilon = 1e-08

DOM, NY, NX, NC = 12, 8, 4, 2
D = 400
WIDE = 512
SHARD = 16
META = 8
PAY = SHARD + META
SLOTS = 512
LANES = 128
HALF = NX * NY
HI = lax.Precision.HIGHEST
NT = (((1,), (1,)), ((), ()))
TN = (((0,), (0,)), ((), ()))


def whole(space=pltpu.VMEM):
    return pl.BlockSpec(memory_space=space)


def pack_kernel(count_ref, emb_ref, src_ref, dst_ref, neg_ref, out_ref):
    out_ref[...] = jnp.zeros_like(out_ref)
    out_ref[0:SHARD, 0:D] = emb_ref[...]
    slot = lax.broadcasted_iota(jnp.int32, (1, SLOTS), 1)
    src = jnp.where(slot < count_ref[0], src_ref[...], -1)
    dst, neg = dst_ref[...], neg_ref[...]
    place = (((dst >> 4) & 1) << 9) | (((dst >> 5) & 3) << 7) | ((dst >> 7) << 4) | (dst & 15)
    high = lax.broadcasted_iota(jnp.int32, (8, SLOTS), 0)
    low = lax.broadcasted_iota(jnp.int32, (LANES, SLOTS), 0)
    uses = lax.dot_general(
        jnp.where((neg >> 7) == high, 1.0, 0.0),
        jnp.where((neg & 127) == low, 1.0, 0.0),
        NT,
        precision=HI,
        preferred_element_type=jnp.float32,
    )
    uses = jnp.concatenate([uses[r : r + 1] for r in range(4)], axis=1)
    table = lax.dot_general(
        jnp.where((place >> 7) == high, uses, 0.0),
        jnp.where((place & 127) == low, 1.0, 0.0),
        NT,
        precision=HI,
        preferred_element_type=jnp.float32,
    )
    out_ref[SHARD:PAY, 0:LANES] = table
    src, place = src.astype(jnp.float32), place.astype(jnp.float32)
    for r in range(4):
        cut = slice(r * LANES, (r + 1) * LANES)
        out_ref[SHARD + r : SHARD + r + 1, LANES : 2 * LANES] = src[:, cut]
        out_ref[SHARD + 4 + r : SHARD + 5 + r, LANES : 2 * LANES] = place[:, cut]


def pair_kernel(where_ref, left_ref, own_ref, oth_ref, dleft_ref, down_ref, doth_ref, m_ref):
    worker, core = where_ref[0], where_ref[1]
    left = left_ref[...]

    def rows(ref):
        return ref[:, 0:SHARD, :].reshape(HALF * SHARD, WIDE)

    def dot(a, b, dims=(((1,), (0,)), ((), ()))):
        return lax.dot_general(a, b, dims, precision=HI, preferred_element_type=jnp.float32)

    s_own, s_oth = dot(left, rows(own_ref), NT), dot(left, rows(oth_ref), NT)
    first = core == 0
    s_low = jnp.where(first, s_own, s_oth)
    s_high = jnp.where(first, s_oth, s_own)
    logits = jnp.stack(
        [half[:, r * LANES : (r + 1) * LANES] for half in (s_low, s_high) for r in range(4)]
    )
    m_ref[...] = jnp.zeros_like(m_ref)
    step_rows = lax.broadcasted_iota(jnp.int32, (LANES, SLOTS), 0)

    def over_blocks(ref):
        def block(b, carry):
            meta = ref[b, SHARD:PAY, 0 : 2 * LANES]
            table = meta[:, 0:LANES]
            lists = meta[:, LANES : 2 * LANES].astype(jnp.int32)
            src = jnp.concatenate([lists[r : r + 1] for r in range(4)], axis=1) - worker * SHARD
            dst = jnp.concatenate([lists[r : r + 1] for r in range(4, 8)], axis=1)
            mine = (src >= 0) & (src < SHARD)
            code = jnp.where(mine, ((dst >> 7) << 4) + src, -1)
            at_pair = jnp.where(code == step_rows, 1.0, 0.0).astype(jnp.bfloat16)
            at_low = jnp.where((dst & 127) == step_rows, 1.0, 0.0).astype(jnp.bfloat16)
            edges = lax.dot_general(at_pair, at_low, NT, preferred_element_type=jnp.float32)
            edges = edges.reshape(8, SHARD, LANES)
            counts = jnp.broadcast_to(table[:, None, :], (8, SHARD, LANES))
            masked = jnp.where(counts > 0.0, logits, -jnp.inf)
            top = jnp.max(jnp.max(masked, axis=0), axis=1, keepdims=True)[None]
            weights = counts * jnp.exp(masked - top)
            total = jnp.sum(jnp.sum(weights, axis=0), axis=1, keepdims=True)[None]
            gap = logits - top
            small = jnp.exp(-jnp.abs(gap))
            above = gap >= 0.0
            pos = jnp.where(above, 1.0, small)
            neg = jnp.where(above, small, 1.0)
            share = edges * neg / (pos + total * neg)
            sums = jnp.sum(jnp.sum(share, axis=0), axis=1, keepdims=True)[None]
            m_ref[...] += sums * weights - total * share
            return carry

        lax.fori_loop(0, HALF, block, 0, unroll=2)

    over_blocks(own_ref)
    over_blocks(oth_ref)
    m = m_ref[...]
    m_low = jnp.concatenate([m[r] for r in range(4)], axis=1)
    m_high = jnp.concatenate([m[r] for r in range(4, 8)], axis=1)
    m_own = jnp.where(first, m_low, m_high)
    m_oth = jnp.where(first, m_high, m_low)
    dleft_ref[...] = dot(m_own, rows(own_ref)) + dot(m_oth, rows(oth_ref))
    down_ref[...] = dot(m_own, left, TN)
    doth_ref[...] = dot(m_oth, left, TN)


def to_all(piece, axis, size):
    return lax.all_to_all(jnp.tile(piece, (size, 1)), axis, 0, 0, tiled=True)


def swap_core(piece):
    return lax.ppermute(piece, "c", [(0, 1), (1, 0)])


def summed(piece, axis, size):
    got = lax.all_to_all(piece, axis, 0, 0, tiled=True)
    return jnp.sum(got.reshape(size, -1, got.shape[1]), axis=0)


def body(embeddings, adagrad, plan, src_ids, dst_ids, neg_ids, counts):
    part = lax.axis_index("dom")
    core = lax.axis_index("c")
    worker = (lax.axis_index("y") * NX + lax.axis_index("x")) * NC + core
    sender = jnp.sum(jnp.where(plan == part, jnp.arange(DOM, dtype=jnp.int32), 0))
    f32 = jnp.float32

    own = pl.pallas_call(
        pack_kernel,
        out_shape=jax.ShapeDtypeStruct((PAY, WIDE), f32),
        in_specs=[whole(pltpu.SMEM)] + [whole()] * 4,
        out_specs=whole(),
        name="pack",
    )(counts[0], embeddings, src_ids[0], dst_ids[0], neg_ids[0])

    came = to_all(own, "dom", DOM)
    came = lax.dynamic_slice_in_dim(came, sender * PAY, PAY, 0)
    payload = jnp.concatenate([own[:SHARD], came[SHARD:]], axis=0)
    near = to_all(to_all(payload, "y", NY), "x", NX)
    far = swap_core(near)

    dleft, down, doth = pl.pallas_call(
        pair_kernel,
        out_shape=(
            jax.ShapeDtypeStruct((SHARD, WIDE), f32),
            jax.ShapeDtypeStruct((HALF * SHARD, WIDE), f32),
            jax.ShapeDtypeStruct((HALF * SHARD, WIDE), f32),
        ),
        in_specs=[whole(pltpu.SMEM)] + [whole()] * 3,
        out_specs=(whole(),) * 3,
        scratch_shapes=[pltpu.VMEM((8, SHARD, LANES), f32)],
        compiler_params=pltpu.CompilerParams(vmem_limit_bytes=40 * 1024 * 1024),
        name="pair",
    )(
        jnp.stack([worker, core]).astype(jnp.int32),
        came[:SHARD],
        near.reshape(HALF, PAY, WIDE),
        far.reshape(HALF, PAY, WIDE),
    )

    right = summed(summed(down + swap_core(doth), "x", NX), "y", NY)
    back = to_all(dleft, "dom", DOM)
    back = lax.dynamic_slice_in_dim(back, plan[part] * SHARD, SHARD, 0)
    grads = (right + back)[:, :D]
    new_adagrad = adagrad + jnp.mean(grads * grads, axis=1)
    new_embeddings = embeddings - learn_rate * grads / (jnp.sqrt(new_adagrad)[:, None] + epsilon)
    return (new_embeddings, new_adagrad)


def solution(mesh):
    axes = ("dom", "y", "x", "c")
    grid = Mesh(mesh.devices.reshape(DOM, NY, NX, NC), axes)
    edge = P("dom", ("y", "x", "c"), None)
    in_specs = (P(axes, None), P(axes), P(), edge, edge, edge, P("dom", ("y", "x", "c")))
    out_specs = (P(axes, None), P(axes))
    return jax.shard_map(body, mesh=grid, in_specs=in_specs, out_specs=out_specs, check_vma=False)
```

```python
import jax
import jax.numpy as jnp
from jax import lax
from jax.experimental import pallas as pl
from jax.experimental.pallas import tpu as pltpu
from jax.sharding import Mesh, PartitionSpec as P

learn_rate = 0.1
epsilon = 1e-08

DOM, NY, NX, NC = 12, 8, 4, 2
D = 400
WIDE = 512
SHARD = 16
SLOTS = 512
LANES = 128
HALF = NX * NY
ROWS = HALF * SHARD
BODY = 384
HEAD = D - BODY
HI = lax.Precision.HIGHEST
NN = (((1,), (0,)), ((), ()))
NT = (((1,), (1,)), ((), ()))
TN = (((0,), (0,)), ((), ()))
LEFT = 64
BACK = 56
BIG = 24 * 1024 * 1024


SPACES = {"s": pltpu.SMEM, "v": pltpu.VMEM}
WORKER, CORE, AT_X, SENDER, TARGET = range(5)


def whole(space=pltpu.VMEM):
    return pl.BlockSpec(memory_space=space)


def call(kernel, out, spaces, scratch=(), name=None):
    many = isinstance(out, tuple)
    return pl.pallas_call(
        kernel,
        out_shape=out,
        in_specs=[whole(SPACES[space]) for space in spaces],
        out_specs=(whole(),) * len(out) if many else whole(),
        scratch_shapes=list(scratch),
        compiler_params=pltpu.CompilerParams(vmem_limit_bytes=BIG),
        name=name,
    )


def vmem(*shape):
    return pltpu.VMEM(shape, jnp.float32)


def f32(*shape):
    return jax.ShapeDtypeStruct(shape, jnp.float32)


def hi_dot(a, b, dims=NN):
    return lax.dot_general(a, b, dims, precision=HI, preferred_element_type=jnp.float32)


def pack_kernel(count_ref, emb_ref, ids_ref, left_ref, mine_ref, out_ref):
    for ref in (left_ref, mine_ref):
        ref[...] = jnp.zeros_like(ref)
        ref[0:SHARD, 0:D] = emb_ref[...]
    slot = lax.broadcasted_iota(jnp.int32, (1, SLOTS), 1)
    src = jnp.where(slot < count_ref[0], ids_ref[0:1], -1)
    dst, neg = ids_ref[1:2], ids_ref[2:3]
    place = (((dst >> 4) & 1) << 9) | (((dst >> 5) & 3) << 7) | ((dst >> 7) << 4) | (dst & 15)
    high = lax.broadcasted_iota(jnp.int32, (8, SLOTS), 0)
    low = lax.broadcasted_iota(jnp.int32, (LANES, SLOTS), 0)
    uses = lax.dot_general(
        jnp.where((neg >> 7) == high, 1.0, 0.0),
        jnp.where((neg & 127) == low, 1.0, 0.0),
        NT,
        precision=HI,
        preferred_element_type=jnp.float32,
    )
    row = lax.broadcasted_iota(jnp.int32, (SHARD, LANES), 0)
    lane = lax.broadcasted_iota(jnp.int32, (SHARD, LANES), 1)
    out = jnp.zeros((SHARD, LANES), jnp.float32)
    for t, item in enumerate((src, place, uses)):
        if t < 2:
            item = item.astype(jnp.float32)
            item = [item[:, r * LANES : (r + 1) * LANES] for r in range(4)]
        else:
            item = [item[r : r + 1] for r in range(4)]
        item = jnp.concatenate(item * 4, axis=0)
        begin = HEAD + 32 * t
        inside = (lane >= begin) & (lane < begin + 32)
        for j in range(4):
            moved = pltpu.roll(item, (begin - 32 * j) % LANES, 1)
            out = jnp.where(inside & ((row >> 2) == j), moved, out)
    for z in range(DOM):
        out_ref[z] = out


def join_kernel(place_ref, mine_ref, came_ref, out_ref):
    row = mine_ref[...]
    row = jnp.concatenate([row[:, :BODY], row[:, BODY:] + came_ref[place_ref[SENDER]]], axis=1)
    for y in range(NY):
        out_ref[y] = row


def fill_edges(worker, wire_ref, edge_ref, table_ref, list_ref):
    wire = wire_ref[:, :, BODY:WIDE]
    shape = (HALF, SHARD, LANES)
    group = lax.broadcasted_iota(jnp.int32, shape, 2) >> 5
    kept = group == (lax.broadcasted_iota(jnp.int32, shape, 1) >> 2)
    turned = [
        pltpu.roll(wire.reshape(HALF * SHARD, LANES), (32 * d - HEAD) % LANES, 1).reshape(shape)
        for d in range(4)
    ]
    for t in range(3):
        item = turned[-t % 4]
        for j in range(1, 4):
            item = jnp.where(group == j, turned[(j - t) % 4], item)
        item = jnp.where(kept, item, 0.0)
        item = item[:, 0:8, :] + item[:, 8:16, :]
        list_ref[:, 4 * t : 4 * t + 4, :] = item[:, 0:4, :] + item[:, 4:8, :]
    rows = lax.broadcasted_iota(jnp.int32, (LANES, SLOTS), 0).astype(jnp.float32).astype(jnp.bfloat16)
    eight = lax.broadcasted_iota(jnp.int32, (8, SLOTS), 0)
    one, zero = jnp.bfloat16(1.0), jnp.bfloat16(0.0)

    def block(b, carry):
        lists = list_ref[b].astype(jnp.int32)
        src, dst, uses = (
            jnp.concatenate([lists[4 * t + r : 4 * t + r + 1] for r in range(4)], axis=1)
            for t in range(3)
        )
        src = src - worker * SHARD
        mine = (src >= 0) & (src < SHARD)
        high = dst >> 7
        code = jnp.where(mine, (high << 4) + src, -1).astype(jnp.float32).astype(jnp.bfloat16)
        low = (dst & 127).astype(jnp.float32).astype(jnp.bfloat16)
        at_pair = jnp.where(code == rows, one, zero)
        at_low = jnp.where(low == rows, one, zero)
        here = high == eight
        used = jnp.concatenate(
            [
                jnp.where(here, (uses & 255).astype(jnp.float32), 0.0),
                jnp.where(here, (uses >> 8).astype(jnp.float32), 0.0),
            ],
            axis=0,
        ).astype(jnp.bfloat16)
        both = jnp.concatenate([at_pair, used], axis=0)
        both = lax.dot_general(both, at_low, NT, preferred_element_type=jnp.float32)
        edge_ref[b] = both[0:LANES].reshape(8, SHARD, LANES)
        table_ref[b] = both[LANES : LANES + 8] + 256.0 * both[LANES + 8 : LANES + 16]
        return carry

    lax.fori_loop(0, HALF, block, 0, unroll=HALF)


def edges_kernel(place_ref, wire_ref, edge_ref, table_ref, list_ref):
    fill_edges(place_ref[WORKER], wire_ref, edge_ref, table_ref, list_ref)


def pair_kernel(place_ref, left_ref, own_ref, oth_ref, e0_ref, t0_ref, dleft_ref, keep_ref, send_ref, m_ref, e1_ref, t1_ref, list_ref):

    def rows(ref):
        return ref[...].reshape(ROWS, WIDE)

    fill_edges(place_ref[WORKER], oth_ref, e1_ref, t1_ref, list_ref)
    left = left_ref[...]
    s_own, s_oth = hi_dot(left, rows(own_ref), NT), hi_dot(left, rows(oth_ref), NT)
    first = place_ref[CORE] == 0
    s_low = jnp.where(first, s_own, s_oth)
    s_high = jnp.where(first, s_oth, s_own)
    logits = jnp.stack(
        [half[:, r * LANES : (r + 1) * LANES] for half in (s_low, s_high) for r in range(4)]
    )
    m_ref[...] = jnp.zeros_like(m_ref)

    def over_blocks(edge_ref, table_ref):
        def block(b, carry):
            counts = jnp.broadcast_to(table_ref[b][:, None, :], (8, SHARD, LANES))
            masked = jnp.where(counts > 0.0, logits, -jnp.inf)
            top = jnp.max(jnp.max(masked, axis=0), axis=1, keepdims=True)[None]
            size = jnp.exp(jnp.minimum(logits - top, 88.0))
            weights = counts * size
            total = jnp.sum(jnp.sum(weights, axis=0), axis=1, keepdims=True)[None]
            share = edge_ref[b] / (size + total)
            sums = jnp.sum(jnp.sum(share, axis=0), axis=1, keepdims=True)[None]
            m_ref[...] += sums * weights - total * share
            return carry

        lax.fori_loop(0, HALF, block, 0, unroll=HALF)

    over_blocks(e0_ref, t0_ref)
    over_blocks(e1_ref, t1_ref)
    m = m_ref[...]
    m_low = jnp.concatenate([m[r] for r in range(4)], axis=1)
    m_high = jnp.concatenate([m[r] for r in range(4, 8)], axis=1)
    m_own = jnp.where(first, m_low, m_high)
    m_oth = jnp.where(first, m_high, m_low)
    dleft = hi_dot(m_own, rows(own_ref)) + hi_dot(m_oth, rows(oth_ref))
    tail = dleft[:, BODY:]
    tail = jnp.where(
        lax.broadcasted_iota(jnp.int32, (8, LANES), 1) < HEAD, tail[0:8], pltpu.roll(tail[8:16], HEAD, 1)
    )
    dleft = [dleft[:, r * LANES : (r + 1) * LANES] for r in range(3)] + [tail]
    dleft = jnp.concatenate(dleft, axis=0)
    for z in range(DOM):
        dleft_ref[z] = dleft
    for ref, half in ((keep_ref, m_own), (send_ref, m_oth)):
        for k in range(NX):
            ref[k] = half[:, k * LANES : (k + 1) * LANES]
            ref[NX + k] = left[:, k * LANES : (k + 1) * LANES]


def relay_kernel(place_ref, keep_ref, came_ref, *out_refs):
    for k, out_ref in enumerate(out_refs):
        at = lax.rem(place_ref[AT_X] + k, NX)
        for c, ref in enumerate((keep_ref, came_ref)):
            out_ref[c, 0] = ref[at]
            for r in range(4):
                out_ref[c, 1 + r] = ref[NX + r]


def right_kernel(m0_ref, m1_ref, m2_ref, m3_ref, out_ref):
    refs = [(ref, c) for ref in (m0_ref, m1_ref, m2_ref, m3_ref) for c in range(NC)]
    mix = jnp.concatenate([ref[c, 0] for ref, c in refs], axis=0)
    left = [jnp.concatenate([ref[c, 1 + r] for ref, c in refs], axis=0) for r in range(4)]
    grads = hi_dot(mix, jnp.concatenate(left, axis=1), TN)
    out_ref[...] = grads.reshape(NY, SHARD, WIDE)


def finish_kernel(place_ref, emb_ref, ada_ref, right_ref, back_ref, emb_out, ada_out):
    back = back_ref[place_ref[TARGET]]
    tail = back[3 * SHARD :]
    tail = jnp.concatenate([tail, pltpu.roll(tail, LANES - HEAD, 1)], axis=0)
    back = jnp.concatenate([back[r * SHARD : (r + 1) * SHARD] for r in range(3)] + [tail], axis=1)
    grads = back
    for y in range(NY):
        grads = grads + right_ref[y]
    grads = grads[:, 0:D]
    eye = lax.broadcasted_iota(jnp.int32, (SHARD, SHARD), 0)
    eye = eye == lax.broadcasted_iota(jnp.int32, (SHARD, SHARD), 1)
    column = jnp.sum(jnp.where(eye, ada_ref[...], 0.0), axis=1, keepdims=True)
    column = column + jnp.sum(grads * grads, axis=1, keepdims=True) / D
    ada_out[...] = jnp.sum(jnp.where(eye, column, 0.0), axis=0, keepdims=True)
    emb_out[...] = emb_ref[...] - learn_rate * grads / (jnp.sqrt(column) + epsilon)


def swap_core(piece):
    return lax.ppermute(piece, "c", [(0, 1), (1, 0)])


def exchange(pieces, axis):
    return lax.all_to_all(pieces, axis, 0, 0)


def body(embeddings, adagrad, plan, src_ids, dst_ids, neg_ids, counts):
    part = lax.axis_index("dom")
    core = lax.axis_index("c")
    at_x = lax.axis_index("x")
    worker = (lax.axis_index("y") * NX + at_x) * NC + core
    number = jnp.arange(DOM, dtype=jnp.int32)
    sender = jnp.sum(jnp.where(plan == part, number, 0))
    target = jnp.sum(jnp.where(number == part, plan, 0))
    place = jnp.stack([worker, core, at_x, sender, target]).astype(jnp.int32)

    ids = jnp.concatenate([src_ids[0], dst_ids[0], neg_ids[0]], axis=0)
    left, mine, lists = call(
        pack_kernel,
        (f32(LEFT, WIDE), f32(SHARD, WIDE), f32(DOM, SHARD, LANES)),
        "svv",
        name="pack",
    )(counts[0], embeddings, ids)

    left = lax.all_gather(left, "dom", axis=0, tiled=True)
    left = lax.dynamic_slice_in_dim(left, sender * LEFT, SHARD, 0)
    near = call(join_kernel, f32(NY, SHARD, WIDE), "svv", name="join")(place, mine, exchange(lists, "dom"))
    near = exchange(near, "y").reshape(NY * SHARD, WIDE)
    near = exchange(jnp.broadcast_to(near, (NX, NY * SHARD, WIDE)), "x")
    far = swap_core(near)
    near, far = near.reshape(HALF, SHARD, WIDE), far.reshape(HALF, SHARD, WIDE)

    scratch = [vmem(HALF, 8, SHARD, LANES), vmem(HALF, 8, LANES), vmem(HALF, 12, LANES)]
    edges = call(
        edges_kernel,
        (f32(HALF, 8, SHARD, LANES), f32(HALF, 8, LANES)),
        "sv",
        scratch=scratch[2:],
        name="edges",
    )(place, near)
    dleft, keep, send = call(
        pair_kernel,
        (f32(DOM, BACK, LANES), f32(8, SHARD, LANES), f32(8, SHARD, LANES)),
        "svvvvv",
        scratch=[vmem(8, SHARD, LANES)] + scratch,
        name="pair",
    )(place, left, near, far, *edges)

    back = exchange(dleft, "dom")
    messages = call(relay_kernel, (f32(NC, 5, SHARD, LANES),) * NX, "svv", name="relay")(
        place, keep, swap_core(send)
    )
    messages = [messages[0]] + [
        lax.ppermute(messages[k], "x", [(i, (i + k) % NX) for i in range(NX)]) for k in range(1, NX)
    ]
    right = call(right_kernel, f32(NY, SHARD, WIDE), "vvvv", name="right")(*messages)
    right, back = lax.optimization_barrier((right, back))
    right = exchange(right, "y")
    new_embeddings, new_adagrad = call(
        finish_kernel, (f32(SHARD, D), f32(1, SHARD)), "svvvv", name="finish"
    )(place, embeddings, adagrad[None], right, back)
    return (new_embeddings, new_adagrad[0])


def solution(mesh):
    axes = ("dom", "y", "x", "c")
    grid = Mesh(mesh.devices.reshape(DOM, NY, NX, NC), axes)
    edge = P("dom", ("y", "x", "c"), None)
    in_specs = (P(axes, None), P(axes), P(), edge, edge, edge, P("dom", ("y", "x", "c")))
    out_specs = (P(axes, None), P(axes))
    return jax.shard_map(body, mesh=grid, in_specs=in_specs, out_specs=out_specs, check_vma=False)
```

```python
import jax
import jax.numpy as jnp
from jax import lax
from jax.experimental import pallas as pl
from jax.experimental.pallas import tpu as pltpu
from jax.sharding import Mesh, PartitionSpec as P

learn_rate = 0.1
epsilon = 1e-08

DOM, NY, NX, NC = 12, 8, 4, 2
D = 400
WIDE = 512
SHARD = 16
SLOTS = 512
LANES = 128
HALF = NX * NY
ROWS = HALF * SHARD
BODY = 384
HEAD = D - BODY
HI = lax.Precision.HIGHEST
NN = (((1,), (0,)), ((), ()))
NT = (((1,), (1,)), ((), ()))
TN = (((0,), (0,)), ((), ()))
BACK = 56
BIG = 24 * 1024 * 1024


SPACES = {"s": pltpu.SMEM, "v": pltpu.VMEM, "a": pl.ANY}
WORKER, CORE, AT_X, PART, SENDER, TARGET = range(6)


def whole(space=pltpu.VMEM):
    return pl.BlockSpec(memory_space=space)


def call(kernel, out, spaces, scratch=(), name=None, limit=BIG):
    many = isinstance(out, tuple)
    return pl.pallas_call(
        kernel,
        out_shape=out,
        in_specs=[whole(SPACES[space]) for space in spaces],
        out_specs=(whole(),) * len(out) if many else whole(),
        scratch_shapes=list(scratch),
        compiler_params=pltpu.CompilerParams(vmem_limit_bytes=limit),
        name=name,
    )


def vmem(*shape):
    return pltpu.VMEM(shape, jnp.float32)


def f32(*shape):
    return jax.ShapeDtypeStruct(shape, jnp.float32)


def hi_dot(a, b, dims=NN):
    return lax.dot_general(a, b, dims, precision=HI, preferred_element_type=jnp.float32)


def split(value, parts):
    terms = []
    for _ in range(parts):
        terms.append(value.astype(jnp.bfloat16))
        value = value - terms[-1].astype(jnp.float32)
    return terms


def thin_dot(thin, terms, dims):
    parts, rows = len(terms), thin.shape[0]
    thin = split(thin, parts)
    total = None
    for j in reversed(range(parts)):
        stacked = jnp.concatenate(thin[: parts - j], axis=0)
        product = lax.dot_general(stacked, terms[j], dims, preferred_element_type=jnp.float32)
        for i in reversed(range(parts - j)):
            piece = product[i * rows : (i + 1) * rows]
            total = piece if total is None else total + piece
    return total


def pack_kernel(count_hbm, emb_hbm, src_hbm, dst_hbm, neg_hbm, out_ref, count_ref, mine_ref, emb_ref, src_ref, dst_ref, neg_ref, sems):
    copies = [
        pltpu.make_async_copy(count_hbm, count_ref, sems.at[0]),
        pltpu.make_async_copy(src_hbm.at[0], src_ref, sems.at[1]),
        pltpu.make_async_copy(dst_hbm.at[0], dst_ref, sems.at[2]),
        pltpu.make_async_copy(neg_hbm.at[0], neg_ref, sems.at[3]),
        pltpu.make_async_copy(emb_hbm, emb_ref, sems.at[4]),
    ]
    for copy in copies:
        copy.start()
    mine_ref[...] = jnp.zeros_like(mine_ref)
    for copy in copies:
        copy.wait()
    mine_ref[:, 0:D] = emb_ref[...]
    mine = mine_ref[...]
    slot = lax.broadcasted_iota(jnp.int32, (1, SLOTS), 1)
    src = jnp.where(slot < count_ref[...], src_ref[...], -1)
    dst, neg = dst_ref[...], neg_ref[...]
    place = (((dst >> 4) & 1) << 9) | (((dst >> 5) & 3) << 7) | ((dst >> 7) << 4) | (dst & 15)
    high = lax.broadcasted_iota(jnp.int32, (8, SLOTS), 0)
    low = lax.broadcasted_iota(jnp.int32, (LANES, SLOTS), 0)
    uses = lax.dot_general(
        jnp.where((neg >> 7) == high, 1.0, 0.0),
        jnp.where((neg & 127) == low, 1.0, 0.0),
        NT,
        precision=HI,
        preferred_element_type=jnp.float32,
    )
    row = lax.broadcasted_iota(jnp.int32, (SHARD, LANES), 0)
    lane = lax.broadcasted_iota(jnp.int32, (SHARD, LANES), 1)
    out = mine[:, BODY:]
    for t, item in enumerate((src, place, uses)):
        if t < 2:
            item = item.astype(jnp.float32)
            item = [item[:, r * LANES : (r + 1) * LANES] for r in range(4)]
        else:
            item = [item[r : r + 1] for r in range(4)]
        item = jnp.concatenate(item * 4, axis=0)
        begin = HEAD + 32 * t
        inside = (lane >= begin) & (lane < begin + 32)
        for j in range(4):
            moved = pltpu.roll(item, (begin - 32 * j) % LANES, 1)
            out = jnp.where(inside & ((row >> 2) == j), moved, out)
    out = jnp.concatenate([mine[:, :BODY], out], axis=1)
    for z in range(DOM):
        out_ref[z] = out


def join_kernel(place_ref, came_ref, left_ref, out_ref):
    came, mine = came_ref[place_ref[SENDER]], came_ref[place_ref[PART]]
    ours = lax.broadcasted_iota(jnp.int32, (SHARD, WIDE), 1) < D
    left_ref[...] = jnp.where(ours, came, 0.0)
    row = jnp.where(ours, mine, came)
    for y in range(NY):
        out_ref[y] = row


def fill_edges(worker, wire_ref, edge_ref, table_ref, list_ref):
    wire = wire_ref[:, :, BODY:WIDE]
    shape = (HALF, SHARD, LANES)
    group = lax.broadcasted_iota(jnp.int32, shape, 2) >> 5
    kept = group == (lax.broadcasted_iota(jnp.int32, shape, 1) >> 2)
    turned = [
        pltpu.roll(wire.reshape(HALF * SHARD, LANES), (32 * d - HEAD) % LANES, 1).reshape(shape)
        for d in range(4)
    ]
    for t in range(3):
        item = turned[-t % 4]
        for j in range(1, 4):
            item = jnp.where(group == j, turned[(j - t) % 4], item)
        item = jnp.where(kept, item, 0.0)
        item = item[:, 0:8, :] + item[:, 8:16, :]
        list_ref[:, 4 * t : 4 * t + 4, :] = item[:, 0:4, :] + item[:, 4:8, :]
    rows = lax.broadcasted_iota(jnp.int32, (LANES, SLOTS), 0).astype(jnp.float32).astype(jnp.bfloat16)
    eight = lax.broadcasted_iota(jnp.int32, (8, SLOTS), 0)
    one, zero = jnp.bfloat16(1.0), jnp.bfloat16(0.0)

    def block(b, carry):
        lists = list_ref[b].astype(jnp.int32)
        src, dst, uses = (
            jnp.concatenate([lists[4 * t + r : 4 * t + r + 1] for r in range(4)], axis=1)
            for t in range(3)
        )
        src = src - worker * SHARD
        mine = (src >= 0) & (src < SHARD)
        high = dst >> 7
        code = jnp.where(mine, (high << 4) + src, -1).astype(jnp.float32).astype(jnp.bfloat16)
        low = (dst & 127).astype(jnp.float32).astype(jnp.bfloat16)
        at_pair = jnp.where(code == rows, one, zero)
        at_low = jnp.where(low == rows, one, zero)
        here = high == eight
        used = jnp.concatenate(
            [
                jnp.where(here, (uses & 255).astype(jnp.float32), 0.0),
                jnp.where(here, (uses >> 8).astype(jnp.float32), 0.0),
            ],
            axis=0,
        ).astype(jnp.bfloat16)
        both = jnp.concatenate([at_pair, used], axis=0)
        both = lax.dot_general(both, at_low, NT, preferred_element_type=jnp.float32)
        edge_ref[b] = both[0:LANES].reshape(8, SHARD, LANES)
        table_ref[b] = both[LANES : LANES + 8] + 256.0 * both[LANES + 8 : LANES + 16]
        return carry

    lax.fori_loop(0, HALF, block, 0, unroll=HALF)


def edges_kernel(place_ref, wire_ref, edge_ref, table_ref, list_ref):
    fill_edges(place_ref[WORKER], wire_ref, edge_ref, table_ref, list_ref)


def pair_kernel(place_ref, left_ref, own_ref, oth_ref, e0_ref, t0_ref, dleft_ref, keep_ref, send_ref, m_ref, e1_ref, t1_ref, list_ref):

    def rows(ref):
        return ref[...].reshape(ROWS, WIDE)

    fill_edges(place_ref[WORKER], oth_ref, e1_ref, t1_ref, list_ref)
    left = left_ref[...]
    own, oth = split(rows(own_ref), 3), split(rows(oth_ref), 3)
    s_own, s_oth = thin_dot(left, own, NT), thin_dot(left, oth, NT)
    first = place_ref[CORE] == 0
    s_low = jnp.where(first, s_own, s_oth)
    s_high = jnp.where(first, s_oth, s_own)
    logits = jnp.stack(
        [half[:, r * LANES : (r + 1) * LANES] for half in (s_low, s_high) for r in range(4)]
    )
    m_ref[...] = jnp.zeros_like(m_ref)

    def over_blocks(edge_ref, table_ref):
        def block(b, carry):
            counts = jnp.broadcast_to(table_ref[b][:, None, :], (8, SHARD, LANES))
            masked = jnp.where(counts > 0.0, logits, -jnp.inf)
            top = jnp.max(jnp.max(masked, axis=0), axis=1, keepdims=True)[None]
            size = jnp.exp(jnp.minimum(logits - top, 88.0))
            weights = counts * size
            total = jnp.sum(jnp.sum(weights, axis=0), axis=1, keepdims=True)[None]
            share = edge_ref[b] / (size + total)
            sums = jnp.sum(jnp.sum(share, axis=0), axis=1, keepdims=True)[None]
            m_ref[...] += sums * weights - total * share
            return carry

        lax.fori_loop(0, HALF, block, 0, unroll=HALF)

    over_blocks(e0_ref, t0_ref)
    over_blocks(e1_ref, t1_ref)
    m = m_ref[...]
    m_low = jnp.concatenate([m[r] for r in range(4)], axis=1)
    m_high = jnp.concatenate([m[r] for r in range(4, 8)], axis=1)
    m_own = jnp.where(first, m_low, m_high)
    m_oth = jnp.where(first, m_high, m_low)
    dleft = thin_dot(m_own, own, NN) + thin_dot(m_oth, oth, NN)
    tail = dleft[:, BODY:]
    tail = jnp.where(
        lax.broadcasted_iota(jnp.int32, (8, LANES), 1) < HEAD, tail[0:8], pltpu.roll(tail[8:16], HEAD, 1)
    )
    dleft = [dleft[:, r * LANES : (r + 1) * LANES] for r in range(3)] + [tail]
    dleft = jnp.concatenate(dleft, axis=0)
    for z in range(DOM):
        dleft_ref[z] = dleft
    for ref, half in ((keep_ref, m_own), (send_ref, m_oth)):
        for k in range(NX):
            ref[k] = half[:, k * LANES : (k + 1) * LANES]
            ref[NX + k] = left[:, k * LANES : (k + 1) * LANES]


def relay_kernel(place_ref, keep_ref, came_ref, *out_refs):
    for k, out_ref in enumerate(out_refs):
        at = lax.rem(place_ref[AT_X] + k, NX)
        for c, ref in enumerate((keep_ref, came_ref)):
            out_ref[c, 0] = ref[at]
            for r in range(4):
                out_ref[c, 1 + r] = ref[NX + r]


def right_kernel(m0_ref, m1_ref, m2_ref, m3_ref, out_ref):
    refs = [(ref, c) for ref in (m0_ref, m1_ref, m2_ref, m3_ref) for c in range(NC)]
    mix = jnp.concatenate([ref[c, 0] for ref, c in refs], axis=0)
    left = [jnp.concatenate([ref[c, 1 + r] for ref, c in refs], axis=0) for r in range(4)]
    grads = hi_dot(mix, jnp.concatenate(left, axis=1), TN)
    out_ref[...] = grads.reshape(NY, SHARD, WIDE)


def finish_kernel(place_ref, emb_ref, ada_ref, right_ref, back_ref, emb_out, ada_out):
    back = back_ref[place_ref[TARGET]]
    tail = back[3 * SHARD :]
    tail = jnp.concatenate([tail, pltpu.roll(tail, LANES - HEAD, 1)], axis=0)
    back = jnp.concatenate([back[r * SHARD : (r + 1) * SHARD] for r in range(3)] + [tail], axis=1)
    grads = back
    for y in range(NY):
        grads = grads + right_ref[y]
    grads = grads[:, 0:D]
    eye = lax.broadcasted_iota(jnp.int32, (SHARD, SHARD), 0)
    eye = eye == lax.broadcasted_iota(jnp.int32, (SHARD, SHARD), 1)
    column = jnp.sum(jnp.where(eye, ada_ref[...], 0.0), axis=1, keepdims=True)
    column = column + jnp.sum(grads * grads, axis=1, keepdims=True) / D
    ada_out[...] = jnp.sum(jnp.where(eye, column, 0.0), axis=0, keepdims=True)
    emb_out[...] = emb_ref[...] - learn_rate * grads / (jnp.sqrt(column) + epsilon)


def swap_core(piece):
    return lax.ppermute(piece, "c", [(0, 1), (1, 0)])


def exchange(pieces, axis):
    return lax.all_to_all(pieces, axis, 0, 0)


def body(embeddings, adagrad, plan, src_ids, dst_ids, neg_ids, counts):
    part = lax.axis_index("dom")
    core = lax.axis_index("c")
    at_x = lax.axis_index("x")
    worker = (lax.axis_index("y") * NX + at_x) * NC + core
    number = jnp.arange(DOM, dtype=jnp.int32)
    sender = jnp.sum(jnp.where(plan == part, number, 0))
    target = jnp.sum(jnp.where(number == part, plan, 0))
    place = jnp.stack([worker, core, at_x, part, sender, target]).astype(jnp.int32)

    listed = pltpu.VMEM((1, SLOTS), jnp.int32)
    sent = call(
        pack_kernel,
        f32(DOM, SHARD, WIDE),
        "aaaaa",
        scratch=[pltpu.VMEM((1, 1), jnp.int32), vmem(SHARD, WIDE), vmem(SHARD, D)]
        + [listed, listed, listed, pltpu.SemaphoreType.DMA((5,))],
        name="pack",
        limit=None,
    )(counts, embeddings, src_ids, dst_ids, neg_ids)

    left, near = call(join_kernel, (f32(SHARD, WIDE), f32(NY, SHARD, WIDE)), "sv", name="join")(
        place, exchange(sent, "dom")
    )
    near = exchange(near, "y").reshape(NY * SHARD, WIDE)
    near = exchange(jnp.broadcast_to(near, (NX, NY * SHARD, WIDE)), "x")
    far = swap_core(near)
    near, far = near.reshape(HALF, SHARD, WIDE), far.reshape(HALF, SHARD, WIDE)

    scratch = [vmem(HALF, 8, SHARD, LANES), vmem(HALF, 8, LANES), vmem(HALF, 12, LANES)]
    edges = call(
        edges_kernel,
        (f32(HALF, 8, SHARD, LANES), f32(HALF, 8, LANES)),
        "sv",
        scratch=scratch[2:],
        name="edges",
    )(place, near)
    dleft, keep, send = call(
        pair_kernel,
        (f32(DOM, BACK, LANES), f32(8, SHARD, LANES), f32(8, SHARD, LANES)),
        "svvvvv",
        scratch=[vmem(8, SHARD, LANES)] + scratch,
        name="pair",
    )(place, left, near, far, *edges)

    back = exchange(dleft, "dom")
    messages = call(relay_kernel, (f32(NC, 5, SHARD, LANES),) * NX, "svv", name="relay")(
        place, keep, swap_core(send)
    )
    messages = [messages[0]] + [
        lax.ppermute(messages[k], "x", [(i, (i + k) % NX) for i in range(NX)]) for k in range(1, NX)
    ]
    right = call(right_kernel, f32(NY, SHARD, WIDE), "vvvv", name="right")(*messages)
    right, back = lax.optimization_barrier((right, back))
    right = exchange(right, "y")
    new_embeddings, new_adagrad = call(
        finish_kernel, (f32(SHARD, D), f32(1, SHARD)), "svvvv", name="finish"
    )(place, embeddings, adagrad[None], right, back)
    return (new_embeddings, new_adagrad[0])


def solution(mesh):
    axes = ("dom", "y", "x", "c")
    grid = Mesh(mesh.devices.reshape(DOM, NY, NX, NC), axes)
    edge = P("dom", ("y", "x", "c"), None)
    in_specs = (P(axes, None), P(axes), P(), edge, edge, edge, P("dom", ("y", "x", "c")))
    out_specs = (P(axes, None), P(axes))
    return jax.shard_map(body, mesh=grid, in_specs=in_specs, out_specs=out_specs, check_vma=False)
```

```python
import jax
import jax.numpy as jnp
from jax import lax
from jax.experimental import pallas as pl
from jax.experimental.pallas import tpu as pltpu
from jax.sharding import Mesh, PartitionSpec as P

learn_rate = 0.1
epsilon = 1e-08

DOM, NY, NX, NC = 12, 8, 4, 2
D = 400
WIDE = 512
SHARD = 16
SLOTS = 512
LANES = 128
HALF = NX * NY
ROWS = HALF * SHARD
BODY = 384
HEAD = D - BODY
HI = lax.Precision.HIGHEST
NN = (((1,), (0,)), ((), ()))
NT = (((1,), (1,)), ((), ()))
TN = (((0,), (0,)), ((), ()))
BACK = 56
BIG = 24 * 1024 * 1024


SPACES = {"s": pltpu.SMEM, "v": pltpu.VMEM, "a": pl.ANY}
WORKER, CORE, AT_X, PART, SENDER, TARGET = range(6)


def whole(space=pltpu.VMEM):
    return pl.BlockSpec(memory_space=space)


def call(kernel, out, spaces, scratch=(), name=None, limit=BIG):
    many = isinstance(out, tuple)
    return pl.pallas_call(
        kernel,
        out_shape=out,
        in_specs=[whole(SPACES[space]) for space in spaces],
        out_specs=(whole(),) * len(out) if many else whole(),
        scratch_shapes=list(scratch),
        compiler_params=pltpu.CompilerParams(vmem_limit_bytes=limit),
        name=name,
    )


def vmem(*shape):
    return pltpu.VMEM(shape, jnp.float32)


def f32(*shape):
    return jax.ShapeDtypeStruct(shape, jnp.float32)


def hi_dot(a, b, dims=NN):
    return lax.dot_general(a, b, dims, precision=HI, preferred_element_type=jnp.float32)


def split(value, parts):
    terms = []
    for _ in range(parts):
        terms.append(value.astype(jnp.bfloat16))
        value = value - terms[-1].astype(jnp.float32)
    return terms


def thin_dot(thin, terms, dims):
    parts, rows = len(terms), thin.shape[0]
    thin = split(thin, parts)
    total = None
    for j in reversed(range(parts)):
        stacked = jnp.concatenate(thin[: parts - j], axis=0)
        product = lax.dot_general(stacked, terms[j], dims, preferred_element_type=jnp.float32)
        for i in reversed(range(parts - j)):
            piece = product[i * rows : (i + 1) * rows]
            total = piece if total is None else total + piece
    return total


def narrow(value):
    tail = value[:, BODY:]
    lane = lax.broadcasted_iota(jnp.int32, (8, LANES), 1)
    tail = jnp.where(lane < HEAD, tail[0:8], pltpu.roll(tail[8:16], HEAD, 1))
    return jnp.concatenate([value[:, r * LANES : (r + 1) * LANES] for r in range(3)] + [tail], axis=0)


def widen(value):
    tail = value[3 * SHARD :]
    tail = jnp.concatenate([tail, pltpu.roll(tail, LANES - HEAD, 1)], axis=0)
    return jnp.concatenate([value[r * SHARD : (r + 1) * SHARD] for r in range(3)] + [tail], axis=1)


def pack_kernel(count_hbm, emb_hbm, src_hbm, dst_hbm, neg_hbm, out_ref, count_ref, mine_ref, emb_ref, src_ref, dst_ref, neg_ref, sems):
    copies = [
        pltpu.make_async_copy(count_hbm, count_ref, sems.at[0]),
        pltpu.make_async_copy(src_hbm.at[0], src_ref, sems.at[1]),
        pltpu.make_async_copy(dst_hbm.at[0], dst_ref, sems.at[2]),
        pltpu.make_async_copy(neg_hbm.at[0], neg_ref, sems.at[3]),
        pltpu.make_async_copy(emb_hbm, emb_ref, sems.at[4]),
    ]
    for copy in copies:
        copy.start()
    mine_ref[...] = jnp.zeros_like(mine_ref)
    for copy in copies:
        copy.wait()
    mine_ref[:, 0:D] = emb_ref[...]
    mine = mine_ref[...]
    slot = lax.broadcasted_iota(jnp.int32, (1, SLOTS), 1)
    src = jnp.where(slot < count_ref[...], src_ref[...], -1)
    dst, neg = dst_ref[...], neg_ref[...]
    place = (((dst >> 4) & 1) << 9) | (((dst >> 5) & 3) << 7) | ((dst >> 7) << 4) | (dst & 15)
    high = lax.broadcasted_iota(jnp.int32, (8, SLOTS), 0)
    low = lax.broadcasted_iota(jnp.int32, (LANES, SLOTS), 0)
    uses = lax.dot_general(
        jnp.where((neg >> 7) == high, 1.0, 0.0).astype(jnp.bfloat16),
        jnp.where((neg & 127) == low, 1.0, 0.0).astype(jnp.bfloat16),
        NT,
        preferred_element_type=jnp.float32,
    )
    row = lax.broadcasted_iota(jnp.int32, (SHARD, LANES), 0)
    lane = lax.broadcasted_iota(jnp.int32, (SHARD, LANES), 1)
    out = mine[:, BODY:]
    for t, item in enumerate((src, place, uses)):
        if t < 2:
            item = item.astype(jnp.float32)
            item = [item[:, r * LANES : (r + 1) * LANES] for r in range(4)]
        else:
            item = [item[r : r + 1] for r in range(4)]
        item = jnp.concatenate(item * 4, axis=0)
        begin = HEAD + 32 * t
        inside = (lane >= begin) & (lane < begin + 32)
        for j in range(4):
            moved = pltpu.roll(item, (begin - 32 * j) % LANES, 1)
            out = jnp.where(inside & ((row >> 2) == j), moved, out)
    out = jnp.concatenate([mine[:, :BODY], out], axis=1)
    for z in range(DOM):
        out_ref[z] = out


def join_kernel(place_ref, came_ref, left_ref, out_ref):
    came, mine = came_ref[place_ref[SENDER]], came_ref[place_ref[PART]]
    ours = lax.broadcasted_iota(jnp.int32, (SHARD, WIDE), 1) < D
    left_ref[...] = jnp.where(ours, came, 0.0)
    row = jnp.where(ours, mine, came)
    for y in range(NY):
        out_ref[y] = row


def fill_edges(worker, wire_ref, edge_ref, table_ref, list_ref):
    wire = wire_ref[:, :, BODY:WIDE]
    shape = (HALF, SHARD, LANES)
    group = lax.broadcasted_iota(jnp.int32, shape, 2) >> 5
    kept = group == (lax.broadcasted_iota(jnp.int32, shape, 1) >> 2)
    turned = [
        pltpu.roll(wire.reshape(HALF * SHARD, LANES), (32 * d - HEAD) % LANES, 1).reshape(shape)
        for d in range(4)
    ]
    for t in range(3):
        item = turned[-t % 4]
        for j in range(1, 4):
            item = jnp.where(group == j, turned[(j - t) % 4], item)
        item = jnp.where(kept, item, 0.0)
        item = item[:, 0:8, :] + item[:, 8:16, :]
        list_ref[:, 4 * t : 4 * t + 4, :] = item[:, 0:4, :] + item[:, 4:8, :]
    rows = lax.broadcasted_iota(jnp.int32, (LANES, SLOTS), 0).astype(jnp.float32).astype(jnp.bfloat16)
    eight = lax.broadcasted_iota(jnp.int32, (8, SLOTS), 0)
    one, zero = jnp.bfloat16(1.0), jnp.bfloat16(0.0)

    def block(b, carry):
        lists = list_ref[b].astype(jnp.int32)
        src, dst, uses = (
            jnp.concatenate([lists[4 * t + r : 4 * t + r + 1] for r in range(4)], axis=1)
            for t in range(3)
        )
        src = src - worker * SHARD
        mine = (src >= 0) & (src < SHARD)
        high = dst >> 7
        code = jnp.where(mine, (high << 4) + src, -1).astype(jnp.float32).astype(jnp.bfloat16)
        low = (dst & 127).astype(jnp.float32).astype(jnp.bfloat16)
        at_pair = jnp.where(code == rows, one, zero)
        at_low = jnp.where(low == rows, one, zero)
        here = high == eight
        used = jnp.concatenate(
            [
                jnp.where(here, (uses & 255).astype(jnp.float32), 0.0),
                jnp.where(here, (uses >> 8).astype(jnp.float32), 0.0),
            ],
            axis=0,
        ).astype(jnp.bfloat16)
        both = jnp.concatenate([at_pair, used], axis=0)
        both = lax.dot_general(both, at_low, NT, preferred_element_type=jnp.float32)
        edge_ref[b] = both[0:LANES].reshape(8, SHARD, LANES)
        table_ref[b] = both[LANES : LANES + 8] + 256.0 * both[LANES + 8 : LANES + 16]
        return carry

    lax.fori_loop(0, HALF, block, 0, unroll=HALF)


def edges_kernel(place_ref, wire_ref, edge_ref, table_ref, list_ref):
    fill_edges(place_ref[WORKER], wire_ref, edge_ref, table_ref, list_ref)


def pair_kernel(place_ref, left_ref, own_ref, oth_ref, e0_ref, t0_ref, dleft_ref, keep_ref, send_ref, m_ref, e1_ref, t1_ref, list_ref):

    def rows(ref):
        return ref[...].reshape(ROWS, WIDE)

    fill_edges(place_ref[WORKER], oth_ref, e1_ref, t1_ref, list_ref)
    left = left_ref[...]
    own, oth = split(rows(own_ref), 3), split(rows(oth_ref), 3)
    s_own, s_oth = thin_dot(left, own, NT), thin_dot(left, oth, NT)
    first = place_ref[CORE] == 0
    s_low = jnp.where(first, s_own, s_oth)
    s_high = jnp.where(first, s_oth, s_own)
    logits = jnp.stack(
        [half[:, r * LANES : (r + 1) * LANES] for half in (s_low, s_high) for r in range(4)]
    )
    m_ref[...] = jnp.zeros_like(m_ref)

    def over_blocks(edge_ref, table_ref):
        def block(b, carry):
            counts = jnp.broadcast_to(table_ref[b][:, None, :], (8, SHARD, LANES))
            masked = jnp.where(counts > 0.0, logits, -jnp.inf)
            top = jnp.max(jnp.max(masked, axis=0), axis=1, keepdims=True)[None]
            size = jnp.exp(jnp.minimum(logits - top, 88.0))
            weights = counts * size
            total = jnp.sum(jnp.sum(weights, axis=0), axis=1, keepdims=True)[None]
            share = edge_ref[b] / (size + total)
            sums = jnp.sum(jnp.sum(share, axis=0), axis=1, keepdims=True)[None]
            m_ref[...] += sums * weights - total * share
            return carry

        lax.fori_loop(0, HALF, block, 0, unroll=HALF)

    over_blocks(e0_ref, t0_ref)
    over_blocks(e1_ref, t1_ref)
    m = m_ref[...]
    m_low = jnp.concatenate([m[r] for r in range(4)], axis=1)
    m_high = jnp.concatenate([m[r] for r in range(4, 8)], axis=1)
    m_own = jnp.where(first, m_low, m_high)
    m_oth = jnp.where(first, m_high, m_low)
    dleft = thin_dot(m_own, own, NN) + thin_dot(m_oth, oth, NN)
    dleft = narrow(dleft)
    for z in range(DOM):
        dleft_ref[z] = dleft
    for ref, half in ((keep_ref, m_own), (send_ref, m_oth)):
        for k in range(NX):
            ref[k] = half[:, k * LANES : (k + 1) * LANES]
            ref[NX + k] = left[:, k * LANES : (k + 1) * LANES]


def relay_kernel(place_ref, keep_ref, came_ref, *out_refs):
    for k, out_ref in enumerate(out_refs):
        at = lax.rem(place_ref[AT_X] + k, NX)
        for c, ref in enumerate((keep_ref, came_ref)):
            out_ref[c, 0] = ref[at]
            for r in range(4):
                out_ref[c, 1 + r] = ref[NX + r]


def right_kernel(m0_ref, m1_ref, m2_ref, m3_ref, out_ref):
    refs = [(ref, c) for ref in (m0_ref, m1_ref, m2_ref, m3_ref) for c in range(NC)]
    mix = jnp.concatenate([ref[c, 0] for ref, c in refs], axis=0)
    left = [jnp.concatenate([ref[c, 1 + r] for ref, c in refs], axis=0) for r in range(4)]
    grads = hi_dot(mix, jnp.concatenate(left, axis=1), TN)
    for y in range(NY):
        out_ref[y] = narrow(grads[y * SHARD : (y + 1) * SHARD])


def finish_kernel(place_ref, emb_ref, ada_ref, right_ref, back_ref, emb_out, ada_out):
    grads = back_ref[place_ref[TARGET]]
    for y in range(NY):
        grads = grads + right_ref[y]
    grads = widen(grads)[:, 0:D]
    eye = lax.broadcasted_iota(jnp.int32, (SHARD, SHARD), 0)
    eye = eye == lax.broadcasted_iota(jnp.int32, (SHARD, SHARD), 1)
    column = jnp.sum(jnp.where(eye, ada_ref[...], 0.0), axis=1, keepdims=True)
    column = column + jnp.sum(grads * grads, axis=1, keepdims=True) / D
    ada_out[...] = jnp.sum(jnp.where(eye, column, 0.0), axis=0, keepdims=True)
    emb_out[...] = emb_ref[...] - learn_rate * grads / (jnp.sqrt(column) + epsilon)


def swap_core(piece):
    return lax.ppermute(piece, "c", [(0, 1), (1, 0)])


def exchange(pieces, axis):
    return lax.all_to_all(pieces, axis, 0, 0)


def body(embeddings, adagrad, plan, src_ids, dst_ids, neg_ids, counts):
    part = lax.axis_index("dom")
    core = lax.axis_index("c")
    at_x = lax.axis_index("x")
    worker = (lax.axis_index("y") * NX + at_x) * NC + core
    number = jnp.arange(DOM, dtype=jnp.int32)
    sender = jnp.sum(jnp.where(plan == part, number, 0))
    target = jnp.sum(jnp.where(number == part, plan, 0))
    place = jnp.stack([worker, core, at_x, part, sender, target]).astype(jnp.int32)

    listed = pltpu.VMEM((1, SLOTS), jnp.int32)
    sent = call(
        pack_kernel,
        f32(DOM, SHARD, WIDE),
        "aaaaa",
        scratch=[pltpu.VMEM((1, 1), jnp.int32), vmem(SHARD, WIDE), vmem(SHARD, D)]
        + [listed, listed, listed, pltpu.SemaphoreType.DMA((5,))],
        name="pack",
        limit=None,
    )(counts, embeddings, src_ids, dst_ids, neg_ids)

    left, near = call(join_kernel, (f32(SHARD, WIDE), f32(NY, SHARD, WIDE)), "sv", name="join")(
        place, exchange(sent, "dom")
    )
    near = exchange(near, "y").reshape(NY * SHARD, WIDE)
    near = exchange(jnp.broadcast_to(near, (NX, NY * SHARD, WIDE)), "x")
    far = swap_core(near)
    near, far = near.reshape(HALF, SHARD, WIDE), far.reshape(HALF, SHARD, WIDE)

    scratch = [vmem(HALF, 8, SHARD, LANES), vmem(HALF, 8, LANES), vmem(HALF, 12, LANES)]
    edges = call(
        edges_kernel,
        (f32(HALF, 8, SHARD, LANES), f32(HALF, 8, LANES)),
        "sv",
        scratch=scratch[2:],
        name="edges",
    )(place, near)
    dleft, keep, send = call(
        pair_kernel,
        (f32(DOM, BACK, LANES), f32(8, SHARD, LANES), f32(8, SHARD, LANES)),
        "svvvvv",
        scratch=[vmem(8, SHARD, LANES)] + scratch,
        name="pair",
    )(place, left, near, far, *edges)

    back = exchange(dleft, "dom")
    messages = call(relay_kernel, (f32(NC, 5, SHARD, LANES),) * NX, "svv", name="relay")(
        place, keep, swap_core(send)
    )
    messages = [messages[0]] + [
        lax.ppermute(messages[k], "x", [(i, (i + k) % NX) for i in range(NX)]) for k in range(1, NX)
    ]
    right = call(right_kernel, f32(NY, BACK, LANES), "vvvv", name="right")(*messages)
    right, back = lax.optimization_barrier((right, back))
    right = exchange(right, "y")
    new_embeddings, new_adagrad = call(
        finish_kernel, (f32(SHARD, D), f32(1, SHARD)), "svvvv", name="finish"
    )(place, embeddings, adagrad[None], right, back)
    return (new_embeddings, new_adagrad[0])


def solution(mesh):
    axes = ("dom", "y", "x", "c")
    grid = Mesh(mesh.devices.reshape(DOM, NY, NX, NC), axes)
    edge = P("dom", ("y", "x", "c"), None)
    in_specs = (P(axes, None), P(axes), P(), edge, edge, edge, P("dom", ("y", "x", "c")))
    out_specs = (P(axes, None), P(axes))
    return jax.shard_map(body, mesh=grid, in_specs=in_specs, out_specs=out_specs, check_vma=False)
```

```python
import jax
import jax.numpy as jnp
from jax import lax
from jax.experimental import pallas as pl
from jax.experimental.pallas import tpu as pltpu
from jax.sharding import Mesh, PartitionSpec as P

learn_rate = 0.1
epsilon = 1e-08

DOM, NY, NX, NC = 12, 8, 4, 2
D = 400
WIDE = 512
SHARD = 16
SLOTS = 512
LANES = 128
HALF = NX * NY
ROWS = HALF * SHARD
BODY = 384
HEAD = D - BODY
MARK = HEAD + 96
HI = lax.Precision.HIGHEST
NN = (((1,), (0,)), ((), ()))
NT = (((1,), (1,)), ((), ()))
TN = (((0,), (0,)), ((), ()))
BACK = 56
BIG = 24 * 1024 * 1024


SPACES = {"s": pltpu.SMEM, "v": pltpu.VMEM, "a": pl.ANY}


def whole(space=pltpu.VMEM):
    return pl.BlockSpec(memory_space=space)


def call(kernel, out, spaces, scratch=(), name=None, limit=BIG):
    many = isinstance(out, tuple)
    return pl.pallas_call(
        kernel,
        out_shape=out,
        in_specs=[whole(SPACES[space]) for space in spaces],
        out_specs=(whole(),) * len(out) if many else whole(),
        scratch_shapes=list(scratch),
        compiler_params=pltpu.CompilerParams(vmem_limit_bytes=limit),
        name=name,
    )


def worker_of():
    return (lax.axis_index("y") * NX + lax.axis_index("x")) * NC + lax.axis_index("c")


def vmem(*shape):
    return pltpu.VMEM(shape, jnp.float32)


def f32(*shape):
    return jax.ShapeDtypeStruct(shape, jnp.float32)


def hi_dot(a, b, dims=NN):
    return lax.dot_general(a, b, dims, precision=HI, preferred_element_type=jnp.float32)


def split(value, parts):
    terms = []
    for _ in range(parts):
        terms.append(value.astype(jnp.bfloat16))
        value = value - terms[-1].astype(jnp.float32)
    return terms


def thin_dot(thin, terms, dims):
    parts, rows = len(terms), thin.shape[0]
    thin = split(thin, parts)
    total = None
    for j in reversed(range(parts)):
        stacked = jnp.concatenate(thin[: parts - j], axis=0)
        product = lax.dot_general(stacked, terms[j], dims, preferred_element_type=jnp.float32)
        for i in reversed(range(parts - j)):
            piece = product[i * rows : (i + 1) * rows]
            total = piece if total is None else total + piece
    return total


def narrow(value):
    tail = value[:, BODY:]
    lane = lax.broadcasted_iota(jnp.int32, (8, LANES), 1)
    tail = jnp.where(lane < HEAD, tail[0:8], pltpu.roll(tail[8:16], HEAD, 1))
    return jnp.concatenate([value[:, r * LANES : (r + 1) * LANES] for r in range(3)] + [tail], axis=0)


def widen(value):
    tail = value[3 * SHARD :]
    tail = jnp.concatenate([tail, pltpu.roll(tail, LANES - HEAD, 1)], axis=0)
    return jnp.concatenate([value[r * SHARD : (r + 1) * SHARD] for r in range(3)] + [tail], axis=1)


def pack_kernel(count_hbm, emb_hbm, src_hbm, dst_hbm, neg_hbm, plan_hbm, out_ref, count_ref, mine_ref, emb_ref, src_ref, dst_ref, neg_ref, plan_ref, sems):
    copies = [
        pltpu.make_async_copy(count_hbm, count_ref, sems.at[0]),
        pltpu.make_async_copy(src_hbm.at[0], src_ref, sems.at[1]),
        pltpu.make_async_copy(dst_hbm.at[0], dst_ref, sems.at[2]),
        pltpu.make_async_copy(neg_hbm.at[0], neg_ref, sems.at[3]),
        pltpu.make_async_copy(emb_hbm, emb_ref, sems.at[4]),
        pltpu.make_async_copy(plan_hbm, plan_ref, sems.at[5]),
    ]
    for copy in copies:
        copy.start()
    mine_ref[...] = jnp.zeros_like(mine_ref)
    for copy in copies:
        copy.wait()
    mine_ref[:, 0:D] = emb_ref[...]
    mine = mine_ref[...]
    slot = lax.broadcasted_iota(jnp.int32, (1, SLOTS), 1)
    src = jnp.where(slot < count_ref[...], src_ref[...], -1)
    dst, neg = dst_ref[...], neg_ref[...]
    place = (((dst >> 4) & 1) << 9) | (((dst >> 5) & 3) << 7) | ((dst >> 7) << 4) | (dst & 15)
    high = lax.broadcasted_iota(jnp.int32, (8, SLOTS), 0)
    low = lax.broadcasted_iota(jnp.int32, (LANES, SLOTS), 0)
    uses = lax.dot_general(
        jnp.where((neg >> 7) == high, 1.0, 0.0).astype(jnp.bfloat16),
        jnp.where((neg & 127) == low, 1.0, 0.0).astype(jnp.bfloat16),
        NT,
        preferred_element_type=jnp.float32,
    )
    row = lax.broadcasted_iota(jnp.int32, (SHARD, LANES), 0)
    lane = lax.broadcasted_iota(jnp.int32, (SHARD, LANES), 1)
    target = plan_ref[lax.axis_index("dom")].astype(jnp.float32)
    out = jnp.where(lane < MARK, mine[:, BODY:], target)
    for t, item in enumerate((src, place, uses)):
        if t < 2:
            item = item.astype(jnp.float32)
            item = [item[:, r * LANES : (r + 1) * LANES] for r in range(4)]
        else:
            item = [item[r : r + 1] for r in range(4)]
        item = jnp.concatenate(item * 4, axis=0)
        begin = HEAD + 32 * t
        inside = (lane >= begin) & (lane < begin + 32)
        for j in range(4):
            moved = pltpu.roll(item, (begin - 32 * j) % LANES, 1)
            out = jnp.where(inside & ((row >> 2) == j), moved, out)
    out = jnp.concatenate([mine[:, :BODY], out], axis=1)
    for z in range(DOM):
        out_ref[z] = out


def join_kernel(came_ref, left_ref, out_ref):
    part = lax.axis_index("dom")
    mine, came = came_ref[part], came_ref[0]
    here = part.astype(jnp.float32)
    for z in range(1, DOM):
        block = came_ref[z]
        came = jnp.where(block[:, BODY + MARK : BODY + MARK + 1] == here, block, came)
    ours = lax.broadcasted_iota(jnp.int32, (SHARD, WIDE), 1) < D
    left_ref[...] = jnp.where(ours, came, 0.0)
    row = jnp.where(ours, mine, came)
    for y in range(NY):
        out_ref[y] = row


def fill_edges(worker, wire_ref, edge_ref, table_ref, list_ref):
    wire = wire_ref[:, :, BODY:WIDE]
    shape = (HALF, SHARD, LANES)
    group = lax.broadcasted_iota(jnp.int32, shape, 2) >> 5
    kept = group == (lax.broadcasted_iota(jnp.int32, shape, 1) >> 2)
    turned = [
        pltpu.roll(wire.reshape(HALF * SHARD, LANES), (32 * d - HEAD) % LANES, 1).reshape(shape)
        for d in range(4)
    ]
    for t in range(3):
        item = turned[-t % 4]
        for j in range(1, 4):
            item = jnp.where(group == j, turned[(j - t) % 4], item)
        item = jnp.where(kept, item, 0.0)
        item = item[:, 0:8, :] + item[:, 8:16, :]
        list_ref[:, 4 * t : 4 * t + 4, :] = item[:, 0:4, :] + item[:, 4:8, :]
    rows = lax.broadcasted_iota(jnp.int32, (LANES, SLOTS), 0).astype(jnp.float32).astype(jnp.bfloat16)
    eight = lax.broadcasted_iota(jnp.int32, (8, SLOTS), 0)
    one, zero = jnp.bfloat16(1.0), jnp.bfloat16(0.0)

    def block(b, carry):
        lists = list_ref[b].astype(jnp.int32)
        src, dst, uses = (
            jnp.concatenate([lists[4 * t + r : 4 * t + r + 1] for r in range(4)], axis=1)
            for t in range(3)
        )
        src = src - worker * SHARD
        mine = (src >= 0) & (src < SHARD)
        high = dst >> 7
        code = jnp.where(mine, (high << 4) + src, -1).astype(jnp.float32).astype(jnp.bfloat16)
        low = (dst & 127).astype(jnp.float32).astype(jnp.bfloat16)
        at_pair = jnp.where(code == rows, one, zero)
        at_low = jnp.where(low == rows, one, zero)
        here = high == eight
        used = jnp.concatenate(
            [
                jnp.where(here, (uses & 255).astype(jnp.float32), 0.0),
                jnp.where(here, (uses >> 8).astype(jnp.float32), 0.0),
            ],
            axis=0,
        ).astype(jnp.bfloat16)
        both = jnp.concatenate([at_pair, used], axis=0)
        both = lax.dot_general(both, at_low, NT, preferred_element_type=jnp.float32)
        edge_ref[b] = both[0:LANES].reshape(8, SHARD, LANES)
        table_ref[b] = both[LANES : LANES + 8] + 256.0 * both[LANES + 8 : LANES + 16]
        return carry

    lax.fori_loop(0, HALF, block, 0, unroll=HALF)


def edges_kernel(left_ref, wire_ref, edge_ref, table_ref, logit_ref, list_ref):
    fill_edges(worker_of(), wire_ref, edge_ref, table_ref, list_ref)
    logit_ref[...] = thin_dot(left_ref[...], split(wire_ref[...].reshape(ROWS, WIDE), 3), NT)


def pair_kernel(left_ref, own_ref, oth_ref, e0_ref, t0_ref, s0_ref, dleft_ref, keep_ref, send_ref, m_ref, e1_ref, t1_ref, list_ref):

    def rows(ref):
        return ref[...].reshape(ROWS, WIDE)

    fill_edges(worker_of(), oth_ref, e1_ref, t1_ref, list_ref)
    left = left_ref[...]
    own, oth = split(rows(own_ref), 2), split(rows(oth_ref), 3)
    s_own, s_oth = s0_ref[...], thin_dot(left, oth, NT)
    first = lax.axis_index("c") == 0
    s_low = jnp.where(first, s_own, s_oth)
    s_high = jnp.where(first, s_oth, s_own)
    logits = jnp.stack(
        [half[:, r * LANES : (r + 1) * LANES] for half in (s_low, s_high) for r in range(4)]
    )
    m_ref[...] = jnp.zeros_like(m_ref)

    def over_blocks(edge_ref, table_ref):
        def block(b, carry):
            counts = jnp.broadcast_to(table_ref[b][:, None, :], (8, SHARD, LANES))
            masked = jnp.where(counts > 0.0, logits, -jnp.inf)
            top = jnp.max(jnp.max(masked, axis=0), axis=1, keepdims=True)[None]
            size = jnp.exp(jnp.minimum(logits - top, 88.0))
            weights = counts * size
            total = jnp.sum(jnp.sum(weights, axis=0), axis=1, keepdims=True)[None]
            share = edge_ref[b] / (size + total)
            sums = jnp.sum(jnp.sum(share, axis=0), axis=1, keepdims=True)[None]
            m_ref[...] += sums * weights - total * share
            return carry

        lax.fori_loop(0, HALF, block, 0, unroll=HALF)

    over_blocks(e0_ref, t0_ref)
    over_blocks(e1_ref, t1_ref)
    m = m_ref[...]
    m_low = jnp.concatenate([m[r] for r in range(4)], axis=1)
    m_high = jnp.concatenate([m[r] for r in range(4, 8)], axis=1)
    m_own = jnp.where(first, m_low, m_high)
    m_oth = jnp.where(first, m_high, m_low)
    dleft = thin_dot(m_own, own, NN) + thin_dot(m_oth, oth[:2], NN)
    dleft = narrow(dleft)
    for z in range(DOM):
        dleft_ref[z] = dleft
    for ref, half in ((keep_ref, m_own), (send_ref, m_oth)):
        for k in range(NX):
            ref[k] = half[:, k * LANES : (k + 1) * LANES]
            ref[NX + k] = left[:, k * LANES : (k + 1) * LANES]


def relay_kernel(keep_ref, came_ref, *out_refs):
    for k, out_ref in enumerate(out_refs):
        at = lax.rem(lax.axis_index("x") + k, NX)
        for c, ref in enumerate((keep_ref, came_ref)):
            out_ref[c, 0] = ref[at]
            for r in range(4):
                out_ref[c, 1 + r] = ref[NX + r]


def right_kernel(m0_ref, m1_ref, m2_ref, m3_ref, out_ref):
    refs = [(ref, c) for ref in (m0_ref, m1_ref, m2_ref, m3_ref) for c in range(NC)]
    mix = jnp.concatenate([ref[c, 0] for ref, c in refs], axis=0)
    left = [jnp.concatenate([ref[c, 1 + r] for ref, c in refs], axis=0) for r in range(4)]
    grads = hi_dot(mix, jnp.concatenate(left, axis=1), TN)
    for y in range(NY):
        out_ref[y] = narrow(grads[y * SHARD : (y + 1) * SHARD])


def finish_kernel(plan_ref, emb_ref, ada_ref, right_ref, back_ref, emb_out, ada_out):
    here = lax.broadcasted_iota(jnp.int32, (1, DOM), 1) == lax.axis_index("dom")
    target = jnp.sum(jnp.where(here, plan_ref[...], 0).astype(jnp.float32), axis=1, keepdims=True)
    grads = back_ref[0]
    for z in range(1, DOM):
        grads = jnp.where(target == z, back_ref[z], grads)
    for y in range(NY):
        grads = grads + right_ref[y]
    grads = widen(grads)[:, 0:D]
    eye = lax.broadcasted_iota(jnp.int32, (SHARD, SHARD), 0)
    eye = eye == lax.broadcasted_iota(jnp.int32, (SHARD, SHARD), 1)
    column = jnp.sum(jnp.where(eye, ada_ref[...], 0.0), axis=1, keepdims=True)
    column = column + jnp.sum(grads * grads, axis=1, keepdims=True) / D
    ada_out[...] = jnp.sum(jnp.where(eye, column, 0.0), axis=0, keepdims=True)
    emb_out[...] = emb_ref[...] - learn_rate * grads / (jnp.sqrt(column) + epsilon)


def swap_core(piece):
    return lax.ppermute(piece, "c", [(0, 1), (1, 0)])


def exchange(pieces, axis):
    return lax.all_to_all(pieces, axis, 0, 0)


def body(embeddings, adagrad, plan, src_ids, dst_ids, neg_ids, counts):
    listed = pltpu.VMEM((1, SLOTS), jnp.int32)
    sent = call(
        pack_kernel,
        f32(DOM, SHARD, WIDE),
        "aaaaaa",
        scratch=[pltpu.VMEM((1, 1), jnp.int32), vmem(SHARD, WIDE), vmem(SHARD, D)]
        + [listed, listed, listed, pltpu.SMEM((DOM,), jnp.int32), pltpu.SemaphoreType.DMA((6,))],
        name="pack",
        limit=None,
    )(counts, embeddings, src_ids, dst_ids, neg_ids, plan)

    left, near = call(join_kernel, (f32(SHARD, WIDE), f32(NY, SHARD, WIDE)), "v", name="join")(
        exchange(sent, "dom")
    )
    near = exchange(near, "y").reshape(NY * SHARD, WIDE)
    near = exchange(jnp.broadcast_to(near, (NX, NY * SHARD, WIDE)), "x")
    far = swap_core(near)
    near, far = near.reshape(HALF, SHARD, WIDE), far.reshape(HALF, SHARD, WIDE)

    scratch = [vmem(HALF, 8, SHARD, LANES), vmem(HALF, 8, LANES), vmem(HALF, 12, LANES)]
    edges = call(
        edges_kernel,
        (f32(HALF, 8, SHARD, LANES), f32(HALF, 8, LANES), f32(SHARD, WIDE)),
        "vv",
        scratch=scratch[2:],
        name="edges",
    )(left, near)
    dleft, keep, send = call(
        pair_kernel,
        (f32(DOM, BACK, LANES), f32(8, SHARD, LANES), f32(8, SHARD, LANES)),
        "vvvvvv",
        scratch=[vmem(8, SHARD, LANES)] + scratch,
        name="pair",
    )(left, near, far, *edges)

    back = exchange(dleft, "dom")
    messages = call(relay_kernel, (f32(NC, 5, SHARD, LANES),) * NX, "vv", name="relay")(
        keep, swap_core(send)
    )
    messages = [messages[0]] + [
        lax.ppermute(messages[k], "x", [(i, (i + k) % NX) for i in range(NX)]) for k in range(1, NX)
    ]
    right = call(right_kernel, f32(NY, BACK, LANES), "vvvv", name="right")(*messages)
    right, back = lax.optimization_barrier((right, back))
    right = exchange(right, "y")
    new_embeddings, new_adagrad = call(
        finish_kernel, (f32(SHARD, D), f32(1, SHARD)), "vvvvv", name="finish"
    )(plan[None], embeddings, adagrad[None], right, back)
    return (new_embeddings, new_adagrad[0])


def solution(mesh):
    axes = ("dom", "y", "x", "c")
    grid = Mesh(mesh.devices.reshape(DOM, NY, NX, NC), axes)
    edge = P("dom", ("y", "x", "c"), None)
    in_specs = (P(axes, None), P(axes), P(), edge, edge, edge, P("dom", ("y", "x", "c")))
    out_specs = (P(axes, None), P(axes))
    return jax.shard_map(body, mesh=grid, in_specs=in_specs, out_specs=out_specs, check_vma=False)
```

```python
import jax
import jax.numpy as jnp
from jax import lax
from jax.experimental import pallas as pl
from jax.experimental.pallas import tpu as pltpu
from jax.sharding import Mesh, PartitionSpec as P

learn_rate = 0.1
epsilon = 1e-08

DOM, NY, NX, NC = 12, 8, 4, 2
D = 400
WIDE = 512
SHARD = 16
SLOTS = 512
LANES = 128
HALF = NX * NY
ROWS = HALF * SHARD
BODY = 384
HEAD = D - BODY
MARK = HEAD + 96
HI = lax.Precision.HIGHEST
NN = (((1,), (0,)), ((), ()))
NT = (((1,), (1,)), ((), ()))
TN = (((0,), (0,)), ((), ()))
BACK = 56
BIG = 24 * 1024 * 1024


SPACES = {"s": pltpu.SMEM, "v": pltpu.VMEM, "a": pl.ANY}


def whole(space=pltpu.VMEM):
    return pl.BlockSpec(memory_space=space)


def call(kernel, out, spaces, scratch=(), name=None, limit=BIG):
    many = isinstance(out, tuple)
    return pl.pallas_call(
        kernel,
        out_shape=out,
        in_specs=[whole(SPACES[space]) for space in spaces],
        out_specs=(whole(),) * len(out) if many else whole(),
        scratch_shapes=list(scratch),
        compiler_params=pltpu.CompilerParams(vmem_limit_bytes=limit),
        name=name,
    )


def worker_of():
    return (lax.axis_index("y") * NX + lax.axis_index("x")) * NC + lax.axis_index("c")


def vmem(*shape):
    return pltpu.VMEM(shape, jnp.float32)


def f32(*shape):
    return jax.ShapeDtypeStruct(shape, jnp.float32)


def hi_dot(a, b, dims=NN):
    return lax.dot_general(a, b, dims, precision=HI, preferred_element_type=jnp.float32)


def split(value, parts):
    terms = []
    for _ in range(parts):
        terms.append(value.astype(jnp.bfloat16))
        value = value - terms[-1].astype(jnp.float32)
    return terms


def thin_dot(thin, terms, dims):
    parts, rows = len(terms), thin.shape[0]
    thin = split(thin, parts)
    total = None
    for j in reversed(range(parts)):
        stacked = jnp.concatenate(thin[: parts - j], axis=0)
        product = lax.dot_general(stacked, terms[j], dims, preferred_element_type=jnp.float32)
        for i in reversed(range(parts - j)):
            piece = product[i * rows : (i + 1) * rows]
            total = piece if total is None else total + piece
    return total


def narrow(value):
    tail = value[:, BODY:]
    lane = lax.broadcasted_iota(jnp.int32, (8, LANES), 1)
    tail = jnp.where(lane < HEAD, tail[0:8], pltpu.roll(tail[8:16], HEAD, 1))
    return jnp.concatenate([value[:, r * LANES : (r + 1) * LANES] for r in range(3)] + [tail], axis=0)


def widen(value):
    tail = value[3 * SHARD :]
    tail = jnp.concatenate([tail, pltpu.roll(tail, LANES - HEAD, 1)], axis=0)
    return jnp.concatenate([value[r * SHARD : (r + 1) * SHARD] for r in range(3)] + [tail], axis=1)


def pack_kernel(count_hbm, emb_hbm, src_hbm, dst_hbm, neg_hbm, plan_hbm, out_ref, count_ref, mine_ref, emb_ref, src_ref, dst_ref, neg_ref, plan_ref, sems):
    copies = [
        pltpu.make_async_copy(count_hbm, count_ref, sems.at[0]),
        pltpu.make_async_copy(src_hbm.at[0], src_ref, sems.at[1]),
        pltpu.make_async_copy(dst_hbm.at[0], dst_ref, sems.at[2]),
        pltpu.make_async_copy(neg_hbm.at[0], neg_ref, sems.at[3]),
        pltpu.make_async_copy(emb_hbm, emb_ref, sems.at[4]),
        pltpu.make_async_copy(plan_hbm, plan_ref, sems.at[5]),
    ]
    for copy in copies:
        copy.start()
    mine_ref[...] = jnp.zeros_like(mine_ref)
    for copy in copies:
        copy.wait()
    mine_ref[:, 0:D] = emb_ref[...]
    mine = mine_ref[...]
    slot = lax.broadcasted_iota(jnp.int32, (1, SLOTS), 1)
    src = jnp.where(slot < count_ref[...], src_ref[...], -1)
    dst, neg = dst_ref[...], neg_ref[...]
    place = (((dst >> 4) & 1) << 9) | (((dst >> 5) & 3) << 7) | ((dst >> 7) << 4) | (dst & 15)
    high = lax.broadcasted_iota(jnp.int32, (8, SLOTS), 0)
    low = lax.broadcasted_iota(jnp.int32, (LANES, SLOTS), 0)
    uses = lax.dot_general(
        jnp.where((neg >> 7) == high, 1.0, 0.0).astype(jnp.bfloat16),
        jnp.where((neg & 127) == low, 1.0, 0.0).astype(jnp.bfloat16),
        NT,
        preferred_element_type=jnp.float32,
    )
    row = lax.broadcasted_iota(jnp.int32, (SHARD, LANES), 0)
    lane = lax.broadcasted_iota(jnp.int32, (SHARD, LANES), 1)
    target = plan_ref[lax.axis_index("dom")].astype(jnp.float32)
    out = jnp.where(lane < MARK, mine[:, BODY:], target)
    for t, item in enumerate((src, place, uses)):
        if t < 2:
            item = item.astype(jnp.float32)
            item = [item[:, r * LANES : (r + 1) * LANES] for r in range(4)]
        else:
            item = [item[r : r + 1] for r in range(4)]
        item = jnp.concatenate(item * 4, axis=0)
        begin = HEAD + 32 * t
        inside = (lane >= begin) & (lane < begin + 32)
        for j in range(4):
            moved = pltpu.roll(item, (begin - 32 * j) % LANES, 1)
            out = jnp.where(inside & ((row >> 2) == j), moved, out)
    out = jnp.concatenate([mine[:, :BODY], out], axis=1)
    for z in range(DOM):
        out_ref[z] = out


def join_kernel(came_ref, left_ref, out_ref):
    part = lax.axis_index("dom")
    mine, came = came_ref[part], came_ref[0]
    here = part.astype(jnp.float32)
    for z in range(1, DOM):
        block = came_ref[z]
        came = jnp.where(block[:, BODY + MARK : BODY + MARK + 1] == here, block, came)
    ours = lax.broadcasted_iota(jnp.int32, (SHARD, WIDE), 1) < D
    left_ref[...] = jnp.where(ours, came, 0.0)
    row = jnp.where(ours, mine, came)
    for y in range(NY):
        out_ref[y] = row


def fill_edges(worker, wire_ref, edge_ref, table_ref, list_ref):
    wire = wire_ref[:, :, BODY:WIDE]
    shape = (HALF, SHARD, LANES)
    group = lax.broadcasted_iota(jnp.int32, shape, 2) >> 5
    kept = group == (lax.broadcasted_iota(jnp.int32, shape, 1) >> 2)
    turned = [
        pltpu.roll(wire.reshape(HALF * SHARD, LANES), (32 * d - HEAD) % LANES, 1).reshape(shape)
        for d in range(4)
    ]
    for t in range(3):
        item = turned[-t % 4]
        for j in range(1, 4):
            item = jnp.where(group == j, turned[(j - t) % 4], item)
        item = jnp.where(kept, item, 0.0)
        item = item[:, 0:8, :] + item[:, 8:16, :]
        list_ref[:, 4 * t : 4 * t + 4, :] = item[:, 0:4, :] + item[:, 4:8, :]
    rows = lax.broadcasted_iota(jnp.int32, (LANES, SLOTS), 0).astype(jnp.float32).astype(jnp.bfloat16)
    eight = lax.broadcasted_iota(jnp.int32, (8, SLOTS), 0)
    one, zero = jnp.bfloat16(1.0), jnp.bfloat16(0.0)

    def block(b, carry):
        lists = list_ref[b].astype(jnp.int32)
        src, dst, uses = (
            jnp.concatenate([lists[4 * t + r : 4 * t + r + 1] for r in range(4)], axis=1)
            for t in range(3)
        )
        src = src - worker * SHARD
        mine = (src >= 0) & (src < SHARD)
        high = dst >> 7
        code = jnp.where(mine, (high << 4) + src, -1).astype(jnp.float32).astype(jnp.bfloat16)
        low = (dst & 127).astype(jnp.float32).astype(jnp.bfloat16)
        at_pair = jnp.where(code == rows, one, zero)
        at_low = jnp.where(low == rows, one, zero)
        here = high == eight
        used = jnp.concatenate(
            [
                jnp.where(here, (uses & 255).astype(jnp.float32), 0.0),
                jnp.where(here, (uses >> 8).astype(jnp.float32), 0.0),
            ],
            axis=0,
        ).astype(jnp.bfloat16)
        both = jnp.concatenate([at_pair, used], axis=0)
        both = lax.dot_general(both, at_low, NT, preferred_element_type=jnp.float32)
        edge_ref[b] = both[0:LANES].reshape(8, SHARD, LANES)
        table_ref[b] = both[LANES : LANES + 8] + 256.0 * both[LANES + 8 : LANES + 16]
        return carry

    lax.fori_loop(0, HALF, block, 0, unroll=HALF)


def edges_kernel(left_ref, wire_ref, edge_ref, table_ref, logit_ref, high_ref, low_ref, list_ref):
    fill_edges(worker_of(), wire_ref, edge_ref, table_ref, list_ref)
    terms = split(wire_ref[...].reshape(ROWS, WIDE), 3)
    logit_ref[...] = thin_dot(left_ref[...], terms, NT)
    high_ref[...], low_ref[...] = terms[0], terms[1]


def pair_kernel(left_ref, oth_ref, e0_ref, t0_ref, s0_ref, high_ref, low_ref, dleft_ref, keep_ref, send_ref, m_ref, e1_ref, t1_ref, list_ref):

    def rows(ref):
        return ref[...].reshape(ROWS, WIDE)

    fill_edges(worker_of(), oth_ref, e1_ref, t1_ref, list_ref)
    left = left_ref[...]
    own, oth = [high_ref[...], low_ref[...]], split(rows(oth_ref), 3)
    s_own, s_oth = s0_ref[...], thin_dot(left, oth, NT)
    first = lax.axis_index("c") == 0
    s_low = jnp.where(first, s_own, s_oth)
    s_high = jnp.where(first, s_oth, s_own)
    logits = jnp.stack(
        [half[:, r * LANES : (r + 1) * LANES] for half in (s_low, s_high) for r in range(4)]
    )
    m_ref[...] = jnp.zeros_like(m_ref)

    def over_blocks(edge_ref, table_ref):
        def block(b, carry):
            counts = jnp.broadcast_to(table_ref[b][:, None, :], (8, SHARD, LANES))
            masked = jnp.where(counts > 0.0, logits, -jnp.inf)
            top = jnp.max(jnp.max(masked, axis=0), axis=1, keepdims=True)[None]
            size = jnp.exp(jnp.minimum(logits - top, 88.0))
            weights = counts * size
            total = jnp.sum(jnp.sum(weights, axis=0), axis=1, keepdims=True)[None]
            share = edge_ref[b] / (size + total)
            sums = jnp.sum(jnp.sum(share, axis=0), axis=1, keepdims=True)[None]
            m_ref[...] += sums * weights - total * share
            return carry

        lax.fori_loop(0, HALF, block, 0, unroll=HALF)

    over_blocks(e0_ref, t0_ref)
    over_blocks(e1_ref, t1_ref)
    m = m_ref[...]
    m_low = jnp.concatenate([m[r] for r in range(4)], axis=1)
    m_high = jnp.concatenate([m[r] for r in range(4, 8)], axis=1)
    m_own = jnp.where(first, m_low, m_high)
    m_oth = jnp.where(first, m_high, m_low)
    dleft = thin_dot(m_own, own, NN) + thin_dot(m_oth, oth[:2], NN)
    dleft = narrow(dleft)
    for z in range(DOM):
        dleft_ref[z] = dleft
    for ref, half in ((keep_ref, m_own), (send_ref, m_oth)):
        for k in range(NX):
            ref[k] = half[:, k * LANES : (k + 1) * LANES]
            ref[NX + k] = left[:, k * LANES : (k + 1) * LANES]


def relay_kernel(keep_ref, came_ref, *out_refs):
    for k, out_ref in enumerate(out_refs):
        at = lax.rem(lax.axis_index("x") + k, NX)
        for c, ref in enumerate((keep_ref, came_ref)):
            out_ref[c, 0] = ref[at]
            for r in range(4):
                out_ref[c, 1 + r] = ref[NX + r]


def right_kernel(m0_ref, m1_ref, m2_ref, m3_ref, out_ref):
    refs = [(ref, c) for ref in (m0_ref, m1_ref, m2_ref, m3_ref) for c in range(NC)]
    mix = jnp.concatenate([ref[c, 0] for ref, c in refs], axis=0)
    left = [jnp.concatenate([ref[c, 1 + r] for ref, c in refs], axis=0) for r in range(4)]
    grads = hi_dot(mix, jnp.concatenate(left, axis=1), TN)
    for y in range(NY):
        out_ref[y] = narrow(grads[y * SHARD : (y + 1) * SHARD])


def finish_kernel(plan_ref, emb_ref, ada_ref, right_ref, back_ref, emb_out, ada_out):
    here = lax.broadcasted_iota(jnp.int32, (1, DOM), 1) == lax.axis_index("dom")
    target = jnp.sum(jnp.where(here, plan_ref[...], 0).astype(jnp.float32), axis=1, keepdims=True)
    grads = back_ref[0]
    for z in range(1, DOM):
        grads = jnp.where(target == z, back_ref[z], grads)
    for y in range(NY):
        grads = grads + right_ref[y]
    grads = widen(grads)[:, 0:D]
    eye = lax.broadcasted_iota(jnp.int32, (SHARD, SHARD), 0)
    eye = eye == lax.broadcasted_iota(jnp.int32, (SHARD, SHARD), 1)
    column = jnp.sum(jnp.where(eye, ada_ref[...], 0.0), axis=1, keepdims=True)
    column = column + jnp.sum(grads * grads, axis=1, keepdims=True) / D
    ada_out[...] = jnp.sum(jnp.where(eye, column, 0.0), axis=0, keepdims=True)
    emb_out[...] = emb_ref[...] - learn_rate * grads / (jnp.sqrt(column) + epsilon)


def swap_core(piece):
    return lax.ppermute(piece, "c", [(0, 1), (1, 0)])


def exchange(pieces, axis):
    return lax.all_to_all(pieces, axis, 0, 0)


def body(embeddings, adagrad, plan, src_ids, dst_ids, neg_ids, counts):
    listed = pltpu.VMEM((1, SLOTS), jnp.int32)
    sent = call(
        pack_kernel,
        f32(DOM, SHARD, WIDE),
        "aaaaaa",
        scratch=[pltpu.VMEM((1, 1), jnp.int32), vmem(SHARD, WIDE), vmem(SHARD, D)]
        + [listed, listed, listed, pltpu.SMEM((DOM,), jnp.int32), pltpu.SemaphoreType.DMA((6,))],
        name="pack",
        limit=None,
    )(counts, embeddings, src_ids, dst_ids, neg_ids, plan)

    left, near = call(join_kernel, (f32(SHARD, WIDE), f32(NY, SHARD, WIDE)), "v", name="join")(
        exchange(sent, "dom")
    )
    near = exchange(near, "y").reshape(NY * SHARD, WIDE)
    near = exchange(jnp.broadcast_to(near, (NX, NY * SHARD, WIDE)), "x")
    far = swap_core(near)
    near, far = near.reshape(HALF, SHARD, WIDE), far.reshape(HALF, SHARD, WIDE)

    scratch = [vmem(HALF, 8, SHARD, LANES), vmem(HALF, 8, LANES), vmem(HALF, 12, LANES)]
    edges = call(
        edges_kernel,
        (f32(HALF, 8, SHARD, LANES), f32(HALF, 8, LANES), f32(SHARD, WIDE))
        + (jax.ShapeDtypeStruct((ROWS, WIDE), jnp.bfloat16),) * 2,
        "vv",
        scratch=scratch[2:],
        name="edges",
    )(left, near)
    dleft, keep, send = call(
        pair_kernel,
        (f32(DOM, BACK, LANES), f32(8, SHARD, LANES), f32(8, SHARD, LANES)),
        "vvvvvvv",
        scratch=[vmem(8, SHARD, LANES)] + scratch,
        name="pair",
    )(left, far, *edges)

    back = exchange(dleft, "dom")
    messages = call(relay_kernel, (f32(NC, 5, SHARD, LANES),) * NX, "vv", name="relay")(
        keep, swap_core(send)
    )
    messages = [messages[0]] + [
        lax.ppermute(messages[k], "x", [(i, (i + k) % NX) for i in range(NX)]) for k in range(1, NX)
    ]
    right = call(right_kernel, f32(NY, BACK, LANES), "vvvv", name="right")(*messages)
    right, back = lax.optimization_barrier((right, back))
    right = exchange(right, "y")
    new_embeddings, new_adagrad = call(
        finish_kernel, (f32(SHARD, D), f32(1, SHARD)), "vvvvv", name="finish"
    )(plan[None], embeddings, adagrad[None], right, back)
    return (new_embeddings, new_adagrad[0])


def solution(mesh):
    axes = ("dom", "y", "x", "c")
    grid = Mesh(mesh.devices.reshape(DOM, NY, NX, NC), axes)
    edge = P("dom", ("y", "x", "c"), None)
    in_specs = (P(axes, None), P(axes), P(), edge, edge, edge, P("dom", ("y", "x", "c")))
    out_specs = (P(axes, None), P(axes))
    return jax.shard_map(body, mesh=grid, in_specs=in_specs, out_specs=out_specs, check_vma=False)
```

```python
import jax
import jax.numpy as jnp
from jax import lax
from jax.experimental import pallas as pl
from jax.experimental.pallas import tpu as pltpu
from jax.sharding import Mesh, PartitionSpec as P

learn_rate = 0.1
epsilon = 1e-08

DOM, NY, NX, NC = 12, 8, 4, 2
D = 400
WIDE = 512
SHARD = 16
SLOTS = 512
LANES = 128
HALF = NX * NY
ROWS = HALF * SHARD
BODY = 384
HEAD = D - BODY
MARK = HEAD + 96
HI = lax.Precision.HIGHEST
NN = (((1,), (0,)), ((), ()))
NT = (((1,), (1,)), ((), ()))
TN = (((0,), (0,)), ((), ()))
BACK = 56
BIG = 24 * 1024 * 1024


SPACES = {"s": pltpu.SMEM, "v": pltpu.VMEM, "a": pl.ANY}


def whole(space=pltpu.VMEM):
    return pl.BlockSpec(memory_space=space)


def call(kernel, out, spaces, scratch=(), name=None, limit=BIG):
    many = isinstance(out, tuple)
    return pl.pallas_call(
        kernel,
        out_shape=out,
        in_specs=[whole(SPACES[space]) for space in spaces],
        out_specs=(whole(),) * len(out) if many else whole(),
        scratch_shapes=list(scratch),
        compiler_params=pltpu.CompilerParams(vmem_limit_bytes=limit),
        name=name,
    )


def worker_of():
    return (lax.axis_index("y") * NX + lax.axis_index("x")) * NC + lax.axis_index("c")


def vmem(*shape):
    return pltpu.VMEM(shape, jnp.float32)


def f32(*shape):
    return jax.ShapeDtypeStruct(shape, jnp.float32)


def hi_dot(a, b, dims=NN):
    return lax.dot_general(a, b, dims, precision=HI, preferred_element_type=jnp.float32)


def split(value, parts):
    terms = []
    for _ in range(parts):
        terms.append(value.astype(jnp.bfloat16))
        value = value - terms[-1].astype(jnp.float32)
    return terms


def low_dot(a, b):
    return lax.dot_general(a, b, TN, preferred_element_type=jnp.float32)


def thin_dot(thin, terms, dims):
    parts, rows = len(terms), thin.shape[0]
    thin = split(thin, parts)
    total = None
    for j in reversed(range(parts)):
        stacked = jnp.concatenate(thin[: parts - j], axis=0)
        product = lax.dot_general(stacked, terms[j], dims, preferred_element_type=jnp.float32)
        for i in reversed(range(parts - j)):
            piece = product[i * rows : (i + 1) * rows]
            total = piece if total is None else total + piece
    return total


def narrow(value):
    tail = value[:, BODY:]
    lane = lax.broadcasted_iota(jnp.int32, (8, LANES), 1)
    tail = jnp.where(lane < HEAD, tail[0:8], pltpu.roll(tail[8:16], HEAD, 1))
    return jnp.concatenate([value[:, r * LANES : (r + 1) * LANES] for r in range(3)] + [tail], axis=0)


def widen(value):
    tail = value[3 * SHARD :]
    tail = jnp.concatenate([tail, pltpu.roll(tail, LANES - HEAD, 1)], axis=0)
    return jnp.concatenate([value[r * SHARD : (r + 1) * SHARD] for r in range(3)] + [tail], axis=1)


def pack_kernel(count_hbm, emb_hbm, src_hbm, dst_hbm, neg_hbm, plan_hbm, out_ref, count_ref, mine_ref, emb_ref, src_ref, dst_ref, neg_ref, plan_ref, sems):
    copies = [
        pltpu.make_async_copy(count_hbm, count_ref, sems.at[0]),
        pltpu.make_async_copy(src_hbm.at[0], src_ref, sems.at[1]),
        pltpu.make_async_copy(dst_hbm.at[0], dst_ref, sems.at[2]),
        pltpu.make_async_copy(neg_hbm.at[0], neg_ref, sems.at[3]),
        pltpu.make_async_copy(emb_hbm, emb_ref, sems.at[4]),
        pltpu.make_async_copy(plan_hbm, plan_ref, sems.at[5]),
    ]
    for copy in copies:
        copy.start()
    mine_ref[...] = jnp.zeros_like(mine_ref)
    for copy in copies:
        copy.wait()
    mine_ref[:, 0:D] = emb_ref[...]
    mine = mine_ref[...]
    slot = lax.broadcasted_iota(jnp.int32, (1, SLOTS), 1)
    src = jnp.where(slot < count_ref[...], src_ref[...], -1)
    dst, neg = dst_ref[...], neg_ref[...]
    place = (((dst >> 4) & 1) << 9) | (((dst >> 5) & 3) << 7) | ((dst >> 7) << 4) | (dst & 15)
    high = lax.broadcasted_iota(jnp.int32, (8, SLOTS), 0)
    low = lax.broadcasted_iota(jnp.int32, (LANES, SLOTS), 0)
    uses = lax.dot_general(
        jnp.where((neg >> 7) == high, 1.0, 0.0).astype(jnp.bfloat16),
        jnp.where((neg & 127) == low, 1.0, 0.0).astype(jnp.bfloat16),
        NT,
        preferred_element_type=jnp.float32,
    )
    row = lax.broadcasted_iota(jnp.int32, (SHARD, LANES), 0)
    lane = lax.broadcasted_iota(jnp.int32, (SHARD, LANES), 1)
    target = plan_ref[lax.axis_index("dom")].astype(jnp.float32)
    out = jnp.where(lane < MARK, mine[:, BODY:], target)
    for t, item in enumerate((src, place, uses)):
        if t < 2:
            item = item.astype(jnp.float32)
            item = [item[:, r * LANES : (r + 1) * LANES] for r in range(4)]
        else:
            item = [item[r : r + 1] for r in range(4)]
        item = jnp.concatenate(item * 4, axis=0)
        begin = HEAD + 32 * t
        inside = (lane >= begin) & (lane < begin + 32)
        for j in range(4):
            moved = pltpu.roll(item, (begin - 32 * j) % LANES, 1)
            out = jnp.where(inside & ((row >> 2) == j), moved, out)
    out = jnp.concatenate([mine[:, :BODY], out], axis=1)
    for z in range(DOM):
        out_ref[z] = out


def join_kernel(came_ref, left_ref, out_ref):
    part = lax.axis_index("dom")
    mine, came = came_ref[part], came_ref[0]
    here = part.astype(jnp.float32)
    for z in range(1, DOM):
        block = came_ref[z]
        came = jnp.where(block[:, BODY + MARK : BODY + MARK + 1] == here, block, came)
    ours = lax.broadcasted_iota(jnp.int32, (SHARD, WIDE), 1) < D
    left_ref[...] = jnp.where(ours, came, 0.0)
    row = jnp.where(ours, mine, came)
    for y in range(NY):
        out_ref[y] = row


def fill_edges(worker, wire_ref, edge_ref, table_ref, list_ref):
    wire = wire_ref[:, :, BODY:WIDE]
    shape = (HALF, SHARD, LANES)
    group = lax.broadcasted_iota(jnp.int32, shape, 2) >> 5
    kept = group == (lax.broadcasted_iota(jnp.int32, shape, 1) >> 2)
    turned = [
        pltpu.roll(wire.reshape(HALF * SHARD, LANES), (32 * d - HEAD) % LANES, 1).reshape(shape)
        for d in range(4)
    ]
    for t in range(3):
        item = turned[-t % 4]
        for j in range(1, 4):
            item = jnp.where(group == j, turned[(j - t) % 4], item)
        item = jnp.where(kept, item, 0.0)
        item = item[:, 0:8, :] + item[:, 8:16, :]
        list_ref[:, 4 * t : 4 * t + 4, :] = item[:, 0:4, :] + item[:, 4:8, :]
    rows = lax.broadcasted_iota(jnp.int32, (LANES, SLOTS), 0).astype(jnp.float32).astype(jnp.bfloat16)
    eight = lax.broadcasted_iota(jnp.int32, (8, SLOTS), 0)
    one, zero = jnp.bfloat16(1.0), jnp.bfloat16(0.0)

    def block(b, carry):
        lists = list_ref[b].astype(jnp.int32)
        src, dst, uses = (
            jnp.concatenate([lists[4 * t + r : 4 * t + r + 1] for r in range(4)], axis=1)
            for t in range(3)
        )
        src = src - worker * SHARD
        mine = (src >= 0) & (src < SHARD)
        high = dst >> 7
        code = jnp.where(mine, (high << 4) + src, -1).astype(jnp.float32).astype(jnp.bfloat16)
        low = (dst & 127).astype(jnp.float32).astype(jnp.bfloat16)
        at_pair = jnp.where(code == rows, one, zero)
        at_low = jnp.where(low == rows, one, zero)
        here = high == eight
        used = jnp.concatenate(
            [
                jnp.where(here, (uses & 255).astype(jnp.float32), 0.0),
                jnp.where(here, (uses >> 8).astype(jnp.float32), 0.0),
            ],
            axis=0,
        ).astype(jnp.bfloat16)
        both = jnp.concatenate([at_pair, used], axis=0)
        both = lax.dot_general(both, at_low, NT, preferred_element_type=jnp.float32)
        edge_ref[b] = both[0:LANES].reshape(8, SHARD, LANES)
        table_ref[b] = both[LANES : LANES + 8] + 256.0 * both[LANES + 8 : LANES + 16]
        return carry

    lax.fori_loop(0, HALF, block, 0, unroll=HALF)


def edges_kernel(left_ref, wire_ref, edge_ref, table_ref, logit_ref, list_ref):
    fill_edges(worker_of(), wire_ref, edge_ref, table_ref, list_ref)
    logit_ref[...] = thin_dot(left_ref[...], split(wire_ref[...].reshape(ROWS, WIDE), 3), NT)


def pair_kernel(left_ref, own_ref, oth_ref, e0_ref, t0_ref, s0_ref, dleft_ref, keep_ref, send_ref, m_ref, e1_ref, t1_ref, list_ref):

    def rows(ref):
        return ref[...].reshape(ROWS, WIDE)

    fill_edges(worker_of(), oth_ref, e1_ref, t1_ref, list_ref)
    left = left_ref[...]
    own, oth = split(rows(own_ref), 2), split(rows(oth_ref), 3)
    s_own, s_oth = s0_ref[...], thin_dot(left, oth, NT)
    first = lax.axis_index("c") == 0
    s_low = jnp.where(first, s_own, s_oth)
    s_high = jnp.where(first, s_oth, s_own)
    logits = jnp.stack(
        [half[:, r * LANES : (r + 1) * LANES] for half in (s_low, s_high) for r in range(4)]
    )
    m_ref[...] = jnp.zeros_like(m_ref)

    def over_blocks(edge_ref, table_ref):
        def block(b, carry):
            counts = jnp.broadcast_to(table_ref[b][:, None, :], (8, SHARD, LANES))
            masked = jnp.where(counts > 0.0, logits, -jnp.inf)
            top = jnp.max(jnp.max(masked, axis=0), axis=1, keepdims=True)[None]
            size = jnp.exp(jnp.minimum(logits - top, 88.0))
            weights = counts * size
            total = jnp.sum(jnp.sum(weights, axis=0), axis=1, keepdims=True)[None]
            share = edge_ref[b] / (size + total)
            sums = jnp.sum(jnp.sum(share, axis=0), axis=1, keepdims=True)[None]
            m_ref[...] += sums * weights - total * share
            return carry

        lax.fori_loop(0, HALF, block, 0, unroll=HALF)

    over_blocks(e0_ref, t0_ref)
    over_blocks(e1_ref, t1_ref)
    m = m_ref[...]
    m_low = jnp.concatenate([m[r] for r in range(4)], axis=1)
    m_high = jnp.concatenate([m[r] for r in range(4, 8)], axis=1)
    m_own = jnp.where(first, m_low, m_high)
    m_oth = jnp.where(first, m_high, m_low)
    dleft = thin_dot(m_own, own, NN) + thin_dot(m_oth, oth[:2], NN)
    dleft = narrow(dleft)
    for z in range(DOM):
        dleft_ref[z] = dleft
    for ref, half in ((keep_ref, m_own), (send_ref, m_oth)):
        for k in range(NX):
            ref[k] = half[:, k * LANES : (k + 1) * LANES]
            ref[NX + k] = left[:, k * LANES : (k + 1) * LANES]


def relay_kernel(keep_ref, came_ref, *out_refs):
    for k, out_ref in enumerate(out_refs):
        at = lax.rem(lax.axis_index("x") + k, NX)
        for c, ref in enumerate((keep_ref, came_ref)):
            out_ref[c, 0] = ref[at]
            for r in range(4):
                out_ref[c, 1 + r] = ref[NX + r]


def right_kernel(m0_ref, m1_ref, m2_ref, m3_ref, out_ref):
    refs = [(ref, c) for ref in (m0_ref, m1_ref, m2_ref, m3_ref) for c in range(NC)]
    mix = jnp.concatenate([ref[c, 0] for ref, c in refs], axis=0)
    left = [jnp.concatenate([ref[c, 1 + r] for ref, c in refs], axis=0) for r in range(4)]
    (mix, mix_low), (left, left_low) = split(mix, 2), split(jnp.concatenate(left, axis=1), 2)
    grads = low_dot(mix_low, left) + low_dot(mix, left_low) + low_dot(mix, left)
    for y in range(NY):
        out_ref[y] = narrow(grads[y * SHARD : (y + 1) * SHARD])


def finish_kernel(plan_ref, emb_ref, ada_ref, right_ref, back_ref, emb_out, ada_out):
    here = lax.broadcasted_iota(jnp.int32, (1, DOM), 1) == lax.axis_index("dom")
    target = jnp.sum(jnp.where(here, plan_ref[...], 0).astype(jnp.float32), axis=1, keepdims=True)
    grads = back_ref[0]
    for z in range(1, DOM):
        grads = jnp.where(target == z, back_ref[z], grads)
    for y in range(NY):
        grads = grads + right_ref[y]
    grads = widen(grads)[:, 0:D]
    eye = lax.broadcasted_iota(jnp.int32, (SHARD, SHARD), 0)
    eye = eye == lax.broadcasted_iota(jnp.int32, (SHARD, SHARD), 1)
    column = jnp.sum(jnp.where(eye, ada_ref[...], 0.0), axis=1, keepdims=True)
    column = column + jnp.sum(grads * grads, axis=1, keepdims=True) / D
    ada_out[...] = jnp.sum(jnp.where(eye, column, 0.0), axis=0, keepdims=True)
    emb_out[...] = emb_ref[...] - learn_rate * grads / (jnp.sqrt(column) + epsilon)


def swap_core(piece):
    return lax.ppermute(piece, "c", [(0, 1), (1, 0)])


def exchange(pieces, axis):
    return lax.all_to_all(pieces, axis, 0, 0)


def body(embeddings, adagrad, plan, src_ids, dst_ids, neg_ids, counts):
    listed = pltpu.VMEM((1, SLOTS), jnp.int32)
    sent = call(
        pack_kernel,
        f32(DOM, SHARD, WIDE),
        "aaaaaa",
        scratch=[pltpu.VMEM((1, 1), jnp.int32), vmem(SHARD, WIDE), vmem(SHARD, D)]
        + [listed, listed, listed, pltpu.SMEM((DOM,), jnp.int32), pltpu.SemaphoreType.DMA((6,))],
        name="pack",
        limit=None,
    )(counts, embeddings, src_ids, dst_ids, neg_ids, plan)

    left, near = call(join_kernel, (f32(SHARD, WIDE), f32(NY, SHARD, WIDE)), "v", name="join")(
        exchange(sent, "dom")
    )
    near = exchange(near, "y").reshape(NY * SHARD, WIDE)
    near = exchange(jnp.broadcast_to(near, (NX, NY * SHARD, WIDE)), "x")
    far = swap_core(near)
    near, far = near.reshape(HALF, SHARD, WIDE), far.reshape(HALF, SHARD, WIDE)

    scratch = [vmem(HALF, 8, SHARD, LANES), vmem(HALF, 8, LANES), vmem(HALF, 12, LANES)]
    edges = call(
        edges_kernel,
        (f32(HALF, 8, SHARD, LANES), f32(HALF, 8, LANES), f32(SHARD, WIDE)),
        "vv",
        scratch=scratch[2:],
        name="edges",
    )(left, near)
    dleft, keep, send = call(
        pair_kernel,
        (f32(DOM, BACK, LANES), f32(8, SHARD, LANES), f32(8, SHARD, LANES)),
        "vvvvvv",
        scratch=[vmem(8, SHARD, LANES)] + scratch,
        name="pair",
    )(left, near, far, *edges)

    back = exchange(dleft, "dom")
    messages = call(relay_kernel, (f32(NC, 5, SHARD, LANES),) * NX, "vv", name="relay")(
        keep, swap_core(send)
    )
    messages = [messages[0]] + [
        lax.ppermute(messages[k], "x", [(i, (i + k) % NX) for i in range(NX)]) for k in range(1, NX)
    ]
    right = call(right_kernel, f32(NY, BACK, LANES), "vvvv", name="right")(*messages)
    right, back = lax.optimization_barrier((right, back))
    right = exchange(right, "y")
    new_embeddings, new_adagrad = call(
        finish_kernel, (f32(SHARD, D), f32(1, SHARD)), "vvvvv", name="finish"
    )(plan[None], embeddings, adagrad[None], right, back)
    return (new_embeddings, new_adagrad[0])


def solution(mesh):
    axes = ("dom", "y", "x", "c")
    grid = Mesh(mesh.devices.reshape(DOM, NY, NX, NC), axes)
    edge = P("dom", ("y", "x", "c"), None)
    in_specs = (P(axes, None), P(axes), P(), edge, edge, edge, P("dom", ("y", "x", "c")))
    out_specs = (P(axes, None), P(axes))
    return jax.shard_map(body, mesh=grid, in_specs=in_specs, out_specs=out_specs, check_vma=False)
```
